512 devices in a mesh: node: 8 (over z_lo, x), wide: 64 (over z_hi, y, core).
Axes of the slice: x: 4, y: 8, z: 8 (z_hi: 4, z_lo: 2; z = z_hi * 2 + z_lo), core: 2. Of those that a mesh axis runs over, the one named last changes fastest.
Arguments:
- features: bfloat16 [6144, 2048], P(('node', 'wide')), may hold values from -0.078125 to 0.078125
- weight: bfloat16 [6144, 18432], P('node', 'wide'), may hold values from -6 to 6
- moment_one: float32 [6144, 18432], P('node', 'wide'), may hold values from -6 to 6
- moment_two: float32 [6144, 18432], P('node', 'wide'), may hold values from 0.05 to 1
- cotangent: bfloat16 [2048, 18432], P('node', 'wide'), may hold values from -10 to 10
- new_owner: int32 [8, 64, 24], P('node', 'wide'), may hold values from 0 to 63, as said below
- new_slot: int32 [8, 64, 24], P('node', 'wide'), may hold values from 0 to 27, as said below
Outputs:
- projected: bfloat16 [2048, 18432], P('node', 'wide')
- moved_weight: bfloat16 [8, 1792, 32, 288], P('node', 'wide')
- moved_first: float32 [8, 1792, 32, 288], P('node', 'wide')
- moved_second: float32 [8, 1792, 32, 288], P('node', 'wide')
The draws below stay inside these ranges and needn't reach their ends.
Inputs may be any that keep to these rules, and one draw needn't show every extreme that they name: new_owner[n, w, b] is the wide index that takes tile b of device (n, w). Within one node group no device hands more than 1 tiles to one peer, and each device takes at most 28 tiles; half of the devices take exactly 28, the others 20. `new_slot`: the slots of the tiles that one device takes over are distinct.
All inputs are finite; a program needn't handle non-finite values.
Results may differ from the reference program's by a relative error of at most 0.001.
Values may be sent and summed in bfloat16 or wider, within the bound.
A program may use at most 128 MiB of HBM per device.

```python
import math
import jax
import jax.numpy as jnp
from jax import lax

D = 6144
TILE = 32
Q = 18432
TOKENS = 2048
BLK = 24
CAP = 28
LIGHT = 20
N_NODE = 8
N_WIDE = 64


def route_tables(key):

    def one_group(group_key):
        order_key, turn_key, shuffle_key = jax.random.split(group_key, 3)
        receivers = jax.random.permutation(order_key, N_WIDE).astype(jnp.int32)
        rotation = jax.random.randint(turn_key, (), 0, N_WIDE).astype(jnp.int32)
        entry = jnp.arange(N_WIDE * BLK, dtype=jnp.int32)
        half = N_WIDE // 2
        heavy_total = half * CAP
        rank = jnp.where(entry < heavy_total, entry // CAP, half + (entry - heavy_total) // LIGHT)
        first = jnp.where(entry < heavy_total, rank * CAP, heavy_total + (rank - half) * LIGHT)
        slot = (entry - first).astype(jnp.int32)
        owner = receivers[rank]
        sender = (entry + rotation) % N_WIDE
        order_in = entry // N_WIDE
        shuffle_keys = jax.random.split(shuffle_key, N_WIDE)
        shuffles = jax.vmap(lambda k: jax.random.permutation(k, BLK).astype(jnp.int32))(shuffle_keys)
        tile = shuffles[sender, order_in]
        owners = jnp.zeros((N_WIDE, BLK), jnp.int32).at[sender, tile].set(owner)
        slots = jnp.zeros((N_WIDE, BLK), jnp.int32).at[sender, tile].set(slot)
        return (owners, slots)
    group_keys = jax.vmap(lambda n: jax.random.fold_in(key, n))(jnp.arange(N_NODE))
    return jax.vmap(one_group)(group_keys)


def draw_new_owner(key, part):
    return route_tables(key)[0]


def draw_new_slot(key, part):
    return route_tables(key)[1]


def block_levels(stream_key, extent, cuts, least, high):
    def one(axis_at, shards_of):
        steps = jax.random.uniform(jax.random.fold_in(jax.random.fold_in(stream_key, 6), axis_at), (shards_of,), jnp.float32, least / len(cuts), high / len(cuts))
        return jnp.repeat(jnp.exp(steps), extent[axis_at] // shards_of).reshape((-1,) + (1,) * (len(extent) - axis_at - 1))

    level = one(*cuts[0])
    for cut in cuts[1:]:
        level = level * one(*cut)
    return level


def noise(key, extent, deviation, most, cuts=(), kind=jnp.bfloat16):
    entries = jax.random.normal(key, extent, jnp.float32) * deviation
    if len(cuts) > 0:
        entries = block_levels(key, extent, cuts, -0.22, 0.18) * entries
    return jnp.clip(entries, min=-most, max=most).astype(kind)


def setup_inputs(seed: int = 0) -> dict:
    seeds = jax.random.split(jax.random.key(seed), 8)
    return {
        "features": noise(seeds[0], (D, TOKENS), (D ** -0.5), 0.078125, ((0, 512),)),
        "weight": noise(seeds[1], (D, Q), 1.0, 6.0, ((0, 8), (1, 64))),
        "moment_one": noise(seeds[2], (D, Q), 1.0, 6.0, ((0, 8), (1, 64)), jnp.float32),
        "moment_two": jnp.clip(jnp.exp(math.log(1.0) - 2.9957323 * jax.random.uniform(seeds[3], (D, Q), jnp.float32) ** block_levels(seeds[3], (D, Q), ((0, 8), (1, 64)), -0.2, 0.2)), 0.05, 1.0),
        "cotangent": noise(seeds[4], (TOKENS, Q), (D ** 0.5 * TOKENS ** -0.5), 10.0, ((0, 8), (1, 64))),
        "new_owner": draw_new_owner(jax.random.fold_in(seeds[7], 71), 0),
        "new_slot": draw_new_slot(jax.random.fold_in(seeds[7], 71), 0),
    }


rate = 0.02
bias_one = 1.0 - 0.9 ** 10
bias_two = 1.0 - 0.999 ** 10

def adam_tiles(grad, weight, first, second):
    g = grad.astype(jnp.float32)
    first_new = 0.9 * first + 0.1 * g
    second_new = 0.999 * second + 0.001 * g * g
    update = first_new / bias_one / (jnp.sqrt(second_new / bias_two) + 1e-08)
    weight_new = (weight.astype(jnp.float32) - rate * update).astype(jnp.bfloat16)
    return (weight_new, first_new, second_new)

def to_tiles(block):
    rows = block.shape[0] // TILE
    width = block.shape[1] // N_WIDE
    tiles = block.reshape(rows, TILE, N_WIDE, width)
    tiles = jnp.transpose(tiles, (2, 0, 1, 3))
    return tiles.reshape(N_WIDE * rows, TILE, width)

def scatter_tiles(tiles, dest):
    empty = jnp.zeros((N_WIDE * CAP, TILE, tiles.shape[2]), tiles.dtype)
    return empty.at[dest].set(tiles)

def reference(features, weight, moment_one, moment_two, cotangent, new_owner, new_slot):
    d_node = D // N_NODE

    def one_node(total, index):
        start = (index * d_node).astype(jnp.int32)
        feat = lax.dynamic_slice_in_dim(features, start, d_node, 0)
        wblock = lax.dynamic_slice_in_dim(weight, start, d_node, 0)
        fblock = lax.dynamic_slice_in_dim(moment_one, start, d_node, 0)
        sblock = lax.dynamic_slice_in_dim(moment_two, start, d_node, 0)
        partial_value = lax.dot_general(feat, wblock, (((0,), (0,)), ((), ())), preferred_element_type=jnp.float32)
        grad = jnp.dot(feat, cotangent, preferred_element_type=jnp.float32).astype(jnp.bfloat16)
        w_new, f_new, s_new = adam_tiles(grad, wblock, fblock, sblock)
        dest = (new_owner[index] * CAP + new_slot[index]).reshape(-1).astype(jnp.int32)
        outs = (scatter_tiles(to_tiles(w_new), dest), scatter_tiles(to_tiles(f_new), dest), scatter_tiles(to_tiles(s_new), dest))
        return (total + partial_value, outs)
    init = jnp.zeros((TOKENS, Q), jnp.float32)
    total, stacked = lax.scan(one_node, init, jnp.arange(N_NODE, dtype=jnp.int32))
    return (total.astype(jnp.bfloat16), stacked[0], stacked[1], stacked[2])
```

```python
import jax
import jax.numpy as jnp
from jax import lax
from jax.experimental import pallas as pl
from jax.experimental.pallas import tpu as pltpu
from jax.sharding import PartitionSpec as P

TILE = 32
NZ, NY, NC = 4, 8, 2
NX = 4
NN = 2 * NX
MESH = pl.DeviceIdType.MESH
ANY = pl.BlockSpec(memory_space=pl.ANY)
HBM = pl.BlockSpec(memory_space=pltpu.HBM)
VMEM = pl.BlockSpec(memory_space=pltpu.VMEM)
SMEM = pl.BlockSpec(memory_space=pltpu.SMEM)
DMA = pltpu.SemaphoreType.DMA

rate = 0.02
bias_one = 1.0 - 0.9**10
bias_two = 1.0 - 0.999**10

TOP = 32767.0
LEAST = 2.0**-100


def place_of(w):
    return w // (NY * NC), (w // NC) % NY, w % NC


def node_peers_of(n, w):
    x = lax.rem(n, NX)
    base = n - x
    return (lax.rem(n + NX, NN), w), [(base + lax.rem(x + k, NX), w) for k in range(1, NX)]


HEAD = 1024
KEEP = 1536


def gather_kernel(
    owner_ref, slot_ref, x_in, c_in, wt_in, onet_in, twot_in,
    a_ref, b_ref, t_ref, call_ref, w_ref, one_ref, two_ref,
    x_ref, wt_ref, onet_ref, twot_ref,
    zs, zr, rs, rr, ls, lr, ss, sr, bs, br, bzs, bzr, bss, bsr,
    ts, tr, tzs, tzr, tss, tsr, ns, nr, loc,
):
    n = lax.axis_index("node")
    w = lax.axis_index("wide")
    z, y, c = place_of(w)

    def wide(zz, yy, cc):
        return (n, (lax.rem(zz + NZ, NZ) * NY + lax.rem(yy + NY, NY)) * NC + cc)

    sibling = wide(z, y, 1 - c)
    y_peers = [wide(z, y + k, c) for k in range(1, NY)]
    right, left = y_peers[0], y_peers[-1]
    z_peers = [wide(z + k, y, c) for k in range(1, NZ)]
    partner, x_peers = node_peers_of(n, w)

    barrier = pltpu.get_barrier_semaphore()
    peers = [sibling, partner] + y_peers + z_peers + x_peers
    for peer in peers:
        pl.semaphore_signal(barrier, inc=1, device_id=peer, device_id_type=MESH)

    own = [
        pltpu.make_async_copy(src, dst, loc.at[i])
        for i, (src, dst) in enumerate((
            (x_in, x_ref), (c_in, call_ref.at[n]),
            (onet_in, onet_ref), (twot_in, twot_ref), (wt_in, wt_ref),
        ))
    ]
    for copy in own:
        copy.start()
    t_ref[z, y, c, 0:1, :owner_ref.shape[1]] = owner_ref[...]
    t_ref[z, y, c, 1:2, :slot_ref.shape[1]] = slot_ref[...]
    own[0].wait()

    rows = x_ref.shape[0]
    extra = (x_ref.shape[1] - KEEP)
    a_ref[z, y, c, :rows, :] = x_ref[:, :HEAD]
    b_ref[z, y, c, :rows, :] = x_ref[:, HEAD:KEEP]
    for k in range(HEAD // extra):
        a_ref[z, y, c, rows:, k * extra:(k + 1) * extra] = x_ref[4 * k:4 * k + 4, KEEP:]
    b_ref[z, y, c, rows:, :] = x_ref[rows - 4:, KEEP:]
    own[1].wait()

    pl.semaphore_wait(barrier, len(peers))

    def send(ref, s, r, peer):
        copy = pltpu.make_async_remote_copy(
            src_ref=ref, dst_ref=ref, send_sem=s, recv_sem=r,
            device_id=peer, device_id_type=MESH,
        )
        copy.start()
        return copy

    z_copies = [
        send(a_ref.at[z, y, c], zs.at[k], zr.at[k], z_peers[k]) for k in range(NZ - 1)
    ]
    b_copies = [
        send(b_ref.at[z, y, c], bs.at[k], br.at[k], y_peers[k]) for k in range(NY - 1)
    ]
    across = send(call_ref.at[n], ns.at[0], nr.at[0], partner)
    x_copies = [
        send(call_ref.at[n], ns.at[k + 1], nr.at[k + 1], x_peers[k]) for k in range(NX - 1)
    ]
    t_copies = [
        send(t_ref.at[z, y, c], ts.at[k], tr.at[k], y_peers[k]) for k in range(NY - 1)
    ]

    def block(k, yy):
        return a_ref.at[lax.rem(z + k, NZ), lax.rem(yy + NY, NY), c]

    half = NY // 2
    order = (0, NZ - 1, 1, 2)
    from_left, from_right, to_sib = {}, {}, []
    for s in range(half + 1):
        for i, k in enumerate(order):
            if s == 0:
                if k > 0:
                    z_copies[NZ - k - 1].wait_recv()
            else:
                if (s - 1, k) in from_left:
                    from_left[s - 1, k].wait_recv()
                if (s - 1, k) in from_right:
                    from_right[s - 1, k].wait_recv()
            if s < half:
                last = s == half - 1
                if not last or i % 2 == 0:
                    from_left[s, k] = send(block(k, y - s), rs.at[s, k], rr.at[s, k], right)
                if not last or i % 2 == 1:
                    from_right[s, k] = send(block(k, y + s), ls.at[s, k], lr.at[s, k], left)
        to_sib.append(send(a_ref.at[:, lax.rem(y - s + NY, NY), c], ss.at[2 * s], sr.at[2 * s], sibling))
        if 0 < s < half:
            to_sib.append(
                send(a_ref.at[:, lax.rem(y + s, NY), c], ss.at[2 * s - 1], sr.at[2 * s - 1], sibling)
            )
        if s == 0:
            for copy in b_copies:
                copy.wait_recv()
            bz = [
                send(b_ref.at[z, :, c], bzs.at[k], bzr.at[k], z_peers[k]) for k in range(NZ - 1)
            ]
            sib_b = [send(b_ref.at[z, :, c], bss.at[0], bsr.at[0], sibling)]
            own[2].wait()
            one_ref[...] = onet_ref[...].T
        if s == 1:
            across.wait_recv()
            other = call_ref.at[lax.rem(n + NX, NN)]
            x_copies += [
                send(other, ns.at[k + NX], nr.at[k + NX], x_peers[k]) for k in range(NX - 1)
            ]
            for copy in t_copies:
                copy.wait_recv()
            tz = [
                send(t_ref.at[z, :, c], tzs.at[k], tzr.at[k], z_peers[k]) for k in range(NZ - 1)
            ]
            sib_t = [send(t_ref.at[z, :, c], tss.at[0], tsr.at[0], sibling)]
            own[3].wait()
            two_ref[...] = twot_ref[...].T
        if s == 2:
            own[4].wait()
            w_ref[...] = wt_ref[...].T
    for k in (NZ - 1, 1, 2):
        at = lax.rem(z + k, NZ)
        bz[NZ - k - 1].wait_recv()
        sib_b.append(send(b_ref.at[at, :, c], bss.at[k], bsr.at[k], sibling))
        tz[NZ - k - 1].wait_recv()
        sib_t.append(send(t_ref.at[at, :, c], tss.at[k], tsr.at[k], sibling))

    for copy in z_copies + b_copies + t_copies + bz + tz + [across]:
        copy.wait_send()
    for copy in list(from_left.values()) + list(from_right.values()):
        copy.wait_send()
    for copy in to_sib + sib_b + sib_t + x_copies:
        copy.wait()


def gather(owners, slots, features, cotangent, wt, onet, twot):
    rows, tokens = features.shape
    cw, ct = cotangent.shape
    width, depth = wt.shape
    half = NY // 2
    pad = rows + rows // 3
    f32, bf16 = jnp.float32, jnp.bfloat16
    a, b, t, call, w, one, two = pl.pallas_call(
        gather_kernel,
        out_shape=(
            jax.ShapeDtypeStruct((NZ, NY, NC, pad, HEAD), bf16),
            jax.ShapeDtypeStruct((NZ, NY, NC, pad, KEEP - HEAD), bf16),
            jax.ShapeDtypeStruct((NZ, NY, NC, 8, 128), jnp.int32),
            jax.ShapeDtypeStruct((NN, cw, ct), bf16),
            jax.ShapeDtypeStruct((depth, width), bf16),
            jax.ShapeDtypeStruct((depth, width), f32),
            jax.ShapeDtypeStruct((depth, width), f32),
        ),
        in_specs=[VMEM] * 2 + [ANY] * 5,
        out_specs=(VMEM,) * 7,
        scratch_shapes=[
            pltpu.VMEM((rows, tokens), bf16),
            pltpu.VMEM((width, depth), bf16),
            pltpu.VMEM((width, depth), f32),
            pltpu.VMEM((width, depth), f32),
            DMA((NZ - 1,)), DMA((NZ - 1,)),
            DMA((half, NZ)), DMA((half, NZ)),
            DMA((half, NZ)), DMA((half, NZ)),
            DMA((NY + 1,)), DMA((NY + 1,)),
            DMA((NY - 1,)), DMA((NY - 1,)),
            DMA((NZ - 1,)), DMA((NZ - 1,)),
            DMA((NZ,)), DMA((NZ,)),
            DMA((NY - 1,)), DMA((NY - 1,)),
            DMA((NZ - 1,)), DMA((NZ - 1,)),
            DMA((NZ,)), DMA((NZ,)),
            DMA((NN - 1,)), DMA((NN - 1,)),
            DMA((5,)),
        ],
        compiler_params=pltpu.CompilerParams(
            collective_id=0, has_side_effects=True, vmem_limit_bytes=32 * 1024 * 1024
        ),
        name="gather_blocks",
    )(
        owners, slots,
        *(pltpu.with_memory_space_constraint(v, pltpu.HBM) for v in (features, cotangent, wt, onet, twot)),
    )
    many = NZ * NY * NC
    a, b, t = (v.reshape((many,) + v.shape[3:]) for v in (a, b, t))
    return a, b, t, call, w, one, two


def project_kernel(a_ref, b_ref, wt_ref, f_ref, own_ref, p1_ref, p2_ref, p3_ref):
    n = lax.axis_index("node")
    x, high = lax.rem(n, NX), n // NX
    blocks, pad, _ = a_ref.shape
    rows = pad * 3 // 4
    tokens = f_ref.shape[1] // NN
    extra = f_ref.shape[1] - KEEP

    def arrange(i, carry):
        at = pl.ds(pl.multiple_of(i * 4 * rows, 16), 4 * rows)
        a = a_ref[pl.ds(4 * i, 4)]
        b = b_ref[pl.ds(4 * i, 4)]
        f_ref[at, :HEAD] = jnp.concatenate([a[j, :rows] for j in range(4)], axis=0)
        f_ref[at, HEAD:KEEP] = jnp.concatenate([b[j, :rows] for j in range(4)], axis=0)
        ends = []
        for j in range(4):
            for k in range(HEAD // extra):
                ends.append(a[j, rows:, k * extra:(k + 1) * extra])
            ends.append(b[j, rows:])
        f_ref[at, KEEP:] = jnp.concatenate(ends, axis=0)
        return carry

    lax.fori_loop(0, blocks // 4, arrange, 0)

    for k, out in ((1, p1_ref), (2, p2_ref), (3, p3_ref), (0, own_ref)):
        for h in range(2):
            node = lax.rem(high + h, 2) * NX + lax.rem(x + k, NX)
            at = pl.ds(pl.multiple_of(node * tokens, tokens), tokens)
            out[h] = jnp.dot(wt_ref[...], f_ref[:, at], preferred_element_type=jnp.float32)


def project(a, b, wt):
    blocks, pad, _ = a.shape
    width, depth = wt.shape
    tokens = KEEP + (KEEP // 3)
    share = jax.ShapeDtypeStruct((2, width, tokens // NN), jnp.float32)
    return pl.pallas_call(
        project_kernel,
        out_shape=(jax.ShapeDtypeStruct((depth, tokens), jnp.bfloat16),) + (share,) * NX,
        in_specs=[VMEM] * 3,
        out_specs=(VMEM,) * (NX + 1),
        compiler_params=pltpu.CompilerParams(vmem_limit_bytes=32 * 1024 * 1024),
        name="arrange_and_project",
    )(a, b, wt)


def sum_shares(own, shares):
    def node(high, x):
        return (high % 2) * NX + x % NX

    came = [
        lax.ppermute(
            share, "node",
            [(node(h, x), node(h, x + k + 1)) for h in range(2) for x in range(NX)],
        )
        for k, share in enumerate(shares)
    ]
    away = own[1] + came[0][1] + came[1][1] + came[2][1]
    across = lax.ppermute(
        away, "node", [(node(h, x), node(h + 1, x)) for h in range(2) for x in range(NX)]
    )
    total = own[0] + came[0][0] + came[1][0] + came[2][0]
    return (total + across).astype(jnp.bfloat16)


def fixed_point(x):
    most = jnp.maximum(jnp.max(jnp.abs(x), axis=1, keepdims=True), LEAST)
    power = jnp.ceil(jnp.log2(most))
    q = jnp.round(x * (TOP * jnp.exp2(-power)))
    return jnp.clip(q, -TOP, TOP).astype(jnp.int32), power.astype(jnp.int32)


def code_of(x):
    a = jnp.abs(x)
    some = a >= 2.0**-126
    safe = jnp.where(some, a, 1.0)
    e = jnp.floor(jnp.log2(safe))
    code = jnp.round((e + 127.0) * 128.0 + (safe * jnp.exp2(-e) - 1.0) * 128.0)
    code = jnp.where(some, code, 0.0)
    return jnp.where(x < 0.0, -code, code).astype(jnp.int32)


def value_of(code):
    a = jnp.abs(code)
    e = lax.shift_right_logical(a, 7)
    m = lax.bitwise_and(a, 127)
    v = (1.0 + m.astype(jnp.float32) * (1.0 / 128.0)) * jnp.exp2(e.astype(jnp.float32) - 127.0)
    v = jnp.where(a == 0, 0.0, v)
    return jnp.where(code < 0, -v, v)


def update_kernel(
    owner_ref, f_ref, c_ref, w_ref, one_ref, two_ref, send_ref, grad, packed, sems
):
    width = w_ref.shape[1]
    full = width // 128 * 128
    rest = width - full
    tail = pl.ds(3 * full, 128)
    part = f_ref.shape[0] // 3

    def put(b):
        return pltpu.make_async_copy(packed.at[b], send_ref.at[owner_ref[b]], sems.at[b])

    def one_tile(b, carry):
        at = pl.ds(pl.multiple_of(b * TILE, TILE), TILE)
        g = grad[at, :]
        first = 0.9 * one_ref[at, :] + 0.1 * g
        second = 0.999 * two_ref[at, :] + 0.001 * g * g
        step = first * (rate / bias_one) / (jnp.sqrt(second * (1.0 / bias_two)) + 1e-08)
        weight = (w_ref[at, :].astype(jnp.float32) - step).astype(jnp.bfloat16)
        qf, pf = fixed_point(first)
        qs, ps = fixed_point(second)
        cw = code_of(weight.astype(jnp.float32))
        packed[b, :, 0:full] = qf[:, :full].astype(jnp.int16)
        packed[b, :, full:2 * full] = qs[:, :full].astype(jnp.int16)
        packed[b, :, 2 * full:3 * full] = cw[:, :full].astype(jnp.int16)
        lane = lax.broadcasted_iota(jnp.int32, (TILE, 128 - 3 * rest), 1)
        powers = jnp.where(lane == 0, pf, ps)
        end = jnp.concatenate([qf[:, full:], qs[:, full:], cw[:, full:], powers], axis=1)
        packed[b, :, tail] = end.astype(jnp.int16)
        put(b).start()
        return carry

    def some(i, carry):
        at = pl.ds(pl.multiple_of(i * part, part), part)
        g = jnp.zeros((part, width), jnp.float32)
        for k in range(c_ref.shape[0]):
            tokens = c_ref.shape[2]
            g += lax.dot_general(
                f_ref[at, k * tokens:(k + 1) * tokens], c_ref[k],
                (((1,), (1,)), ((), ())), preferred_element_type=jnp.float32,
            )
        grad[at, :] = g.astype(jnp.bfloat16).astype(jnp.float32)
        lax.fori_loop(i * (part // TILE), (i + 1) * (part // TILE), one_tile, 0)
        return carry

    lax.fori_loop(0, 3, some, 0)

    def finish(b, carry):
        put(b).wait()
        return carry

    lax.fori_loop(0, owner_ref.shape[0], finish, 0)


def update(owners, rows, cots, weight, one, two, peers):
    depth, width = weight.shape
    lanes = 3 * (width // 128 * 128) + 128
    blocks = depth // TILE
    return pl.pallas_call(
        update_kernel,
        out_shape=pltpu.HBM((peers, TILE, lanes), jnp.int16),
        in_specs=[SMEM] + [VMEM] * 5,
        out_specs=HBM,
        scratch_shapes=[
            pltpu.VMEM((depth, width), jnp.float32),
            pltpu.VMEM((blocks, TILE, lanes), jnp.int16),
            DMA((blocks,)),
        ],
        compiler_params=pltpu.CompilerParams(vmem_limit_bytes=32 * 1024 * 1024),
        name="gradient_and_update",
    )(owners, rows, cots, weight, one, two)


def place_kernel(slot_ref, got_ref, weight_ref, first_ref, second_ref):
    capacity, _, width = weight_ref.shape[1:]
    full = width // 128 * 128
    rest = width - full
    step = pl.program_id(0)
    some = got_ref.shape[0]

    @pl.when(step == 0)
    def _():
        for ref in (weight_ref, first_ref, second_ref):
            ref[...] = jnp.zeros_like(ref)

    def one(p, carry):
        slot = slot_ref[step * some + p]

        @pl.when(slot < capacity)
        def _():
            q = got_ref[p].astype(jnp.int32)
            end = q[:, 3 * full:]
            pf = jnp.exp2(end[:, 3 * rest:3 * rest + 1].astype(jnp.float32)) * (1.0 / TOP)
            ps = jnp.exp2(end[:, 3 * rest + 1:3 * rest + 2].astype(jnp.float32)) * (1.0 / TOP)
            first_ref[0, slot, :, :full] = q[:, :full].astype(jnp.float32) * pf
            first_ref[0, slot, :, full:] = end[:, :rest].astype(jnp.float32) * pf
            second_ref[0, slot, :, :full] = q[:, full:2 * full].astype(jnp.float32) * ps
            second_ref[0, slot, :, full:] = end[:, rest:2 * rest].astype(jnp.float32) * ps
            weight_ref[0, slot, :, :full] = value_of(q[:, 2 * full:3 * full]).astype(jnp.bfloat16)
            weight_ref[0, slot, :, full:] = value_of(end[:, 2 * rest:3 * rest]).astype(jnp.bfloat16)

        return carry

    lax.fori_loop(0, got_ref.shape[0], one, 0)


def place(slots, got, capacity, width):
    shape = (1, capacity, TILE, width)
    return pl.pallas_call(
        place_kernel,
        out_shape=(
            jax.ShapeDtypeStruct(shape, jnp.bfloat16),
            jax.ShapeDtypeStruct(shape, jnp.float32),
            jax.ShapeDtypeStruct(shape, jnp.float32),
        ),
        grid=(8,),
        in_specs=[SMEM, pl.BlockSpec((got.shape[0] // 8,) + got.shape[1:], lambda i: (i, 0, 0))],
        out_specs=(pl.BlockSpec(shape, lambda i: (0, 0, 0, 0)),) * 3,
        compiler_params=pltpu.CompilerParams(vmem_limit_bytes=40 * 1024 * 1024),
        name="place_tiles",
    )(slots, got)


def on_device(features, weight, moment_one, moment_two, cotangent, new_owner, new_slot):
    peers = lax.axis_size("wide")
    owners = new_owner.reshape(-1)
    blocks = owners.shape[0]
    capacity = blocks + blocks // 6
    width = weight.shape[1]
    a, b, tables, cots, weight_rows, one, two = gather(
        new_owner[0], new_slot[0], features, cotangent.T, weight.T, moment_one.T, moment_two.T
    )
    rows, own, *shares = project(a, b, weight.T)
    projected = sum_shares(own, shares).T
    outbox = update(owners, rows, cots, weight_rows, one, two, peers)
    mine = tables[:, 0, :blocks] == lax.axis_index("wide")
    dest = jnp.min(jnp.where(mine, tables[:, 1, :blocks], capacity), axis=1)
    inbox = lax.all_to_all(outbox, "wide", split_axis=0, concat_axis=0, tiled=True)
    moved = place(dest, inbox, capacity, width)
    return (projected,) + tuple(moved)


def solution(mesh):
    placed = (
        P(("node", "wide"), None),
        P("node", "wide"),
        P("node", "wide"),
        P("node", "wide"),
        P("node", "wide"),
        P("node", "wide", None),
        P("node", "wide", None),
    )
    return jax.shard_map(
        on_device,
        mesh=mesh,
        in_specs=placed,
        out_specs=(
            P("node", "wide"),
            P("node", "wide", None, None),
            P("node", "wide", None, None),
            P("node", "wide", None, None),
        ),
        check_vma=False,
    )
```

```python
import jax
import jax.numpy as jnp
from jax import lax
from jax.experimental import pallas as pl
from jax.experimental.pallas import tpu as pltpu
from jax.sharding import PartitionSpec as P

TILE = 32
NZ, NY, NC = 4, 8, 2
NX = 4
NN = 2 * NX
MESH = pl.DeviceIdType.MESH
ANY = pl.BlockSpec(memory_space=pl.ANY)
HBM = pl.BlockSpec(memory_space=pltpu.HBM)
VMEM = pl.BlockSpec(memory_space=pltpu.VMEM)
SMEM = pl.BlockSpec(memory_space=pltpu.SMEM)
DMA = pltpu.SemaphoreType.DMA

rate = 0.02
bias_one = 1.0 - 0.9**10
bias_two = 1.0 - 0.999**10

TOP = 32767.0
LEAST = 2.0**-100


def place_of(w):
    return w // (NY * NC), (w // NC) % NY, w % NC


def node_peers_of(n, w):
    x = lax.rem(n, NX)
    base = n - x
    return (lax.rem(n + NX, NN), w), [(base + lax.rem(x + k, NX), w) for k in range(1, NX)]


HEAD = 1024
KEEP = 1536


def gather_kernel(
    owner_ref, slot_ref, x_in, c_in, wt_in, onet_in, twot_in,
    a_ref, b_ref, t_ref, call_ref, w_ref, one_ref, two_ref,
    x_ref, wt_ref, onet_ref, twot_ref,
    zs, zr, rs, rr, ls, lr, ss, sr, bs, br, bzs, bzr, bss, bsr,
    ts, tr, tzs, tzr, tss, tsr, ns, nr, loc,
):
    n = lax.axis_index("node")
    w = lax.axis_index("wide")
    z, y, c = place_of(w)

    def wide(zz, yy, cc):
        return (n, (lax.rem(zz + NZ, NZ) * NY + lax.rem(yy + NY, NY)) * NC + cc)

    sibling = wide(z, y, 1 - c)
    y_peers = [wide(z, y + k, c) for k in range(1, NY)]
    right, left = y_peers[0], y_peers[-1]
    z_peers = [wide(z + k, y, c) for k in range(1, NZ)]
    partner, x_peers = node_peers_of(n, w)

    barrier = pltpu.get_barrier_semaphore()
    peers = [sibling, partner] + y_peers + z_peers + x_peers
    for peer in peers:
        pl.semaphore_signal(barrier, inc=1, device_id=peer, device_id_type=MESH)

    own = [
        pltpu.make_async_copy(src, dst, loc.at[i])
        for i, (src, dst) in enumerate((
            (x_in, x_ref), (c_in, call_ref.at[n]),
            (onet_in, onet_ref), (twot_in, twot_ref), (wt_in, wt_ref),
        ))
    ]
    for copy in own:
        copy.start()
    t_ref[z, y, c, 0:1, :owner_ref.shape[1]] = owner_ref[...]
    t_ref[z, y, c, 1:2, :slot_ref.shape[1]] = slot_ref[...]
    own[0].wait()

    rows = x_ref.shape[0]
    extra = (x_ref.shape[1] - KEEP)
    a_ref[z, y, c, :rows, :] = x_ref[:, :HEAD]
    b_ref[z, y, c, :rows, :] = x_ref[:, HEAD:KEEP]
    for k in range(HEAD // extra):
        a_ref[z, y, c, rows:, k * extra:(k + 1) * extra] = x_ref[4 * k:4 * k + 4, KEEP:]
    b_ref[z, y, c, rows:, :] = x_ref[rows - 4:, KEEP:]
    own[1].wait()

    pl.semaphore_wait(barrier, len(peers))

    def send(ref, s, r, peer):
        copy = pltpu.make_async_remote_copy(
            src_ref=ref, dst_ref=ref, send_sem=s, recv_sem=r,
            device_id=peer, device_id_type=MESH,
        )
        copy.start()
        return copy

    z_copies = [
        send(a_ref.at[z, y, c], zs.at[k], zr.at[k], z_peers[k]) for k in range(NZ - 1)
    ]
    b_copies = [
        send(b_ref.at[z, y, c], bs.at[k], br.at[k], y_peers[k]) for k in range(NY - 1)
    ]
    across = send(call_ref.at[n], ns.at[0], nr.at[0], partner)
    x_copies = [
        send(call_ref.at[n], ns.at[k + 1], nr.at[k + 1], x_peers[k]) for k in range(NX - 1)
    ]
    t_copies = [
        send(t_ref.at[z, y, c], ts.at[k], tr.at[k], y_peers[k]) for k in range(NY - 1)
    ]

    def block(k, yy):
        return a_ref.at[lax.rem(z + k, NZ), lax.rem(yy + NY, NY), c]

    half = NY // 2
    order = (0, NZ - 1, 1, 2)
    from_left, from_right, to_sib = {}, {}, []
    for s in range(half + 1):
        for i, k in enumerate(order):
            if s == 0:
                if k > 0:
                    z_copies[NZ - k - 1].wait_recv()
            else:
                if (s - 1, k) in from_left:
                    from_left[s - 1, k].wait_recv()
                if (s - 1, k) in from_right:
                    from_right[s - 1, k].wait_recv()
            if s < half:
                last = s == half - 1
                if not last or i % 2 == 0:
                    from_left[s, k] = send(block(k, y - s), rs.at[s, k], rr.at[s, k], right)
                if not last or i % 2 == 1:
                    from_right[s, k] = send(block(k, y + s), ls.at[s, k], lr.at[s, k], left)
        to_sib.append(send(a_ref.at[:, lax.rem(y - s + NY, NY), c], ss.at[2 * s], sr.at[2 * s], sibling))
        if 0 < s < half:
            to_sib.append(
                send(a_ref.at[:, lax.rem(y + s, NY), c], ss.at[2 * s - 1], sr.at[2 * s - 1], sibling)
            )
        if s == 0:
            for copy in b_copies:
                copy.wait_recv()
            bz = [
                send(b_ref.at[z, :, c], bzs.at[k], bzr.at[k], z_peers[k]) for k in range(NZ - 1)
            ]
            sib_b = [send(b_ref.at[z, :, c], bss.at[0], bsr.at[0], sibling)]
            own[2].wait()
            one_ref[...] = onet_ref[...].T
        if s == 1:
            across.wait_recv()
            other = call_ref.at[lax.rem(n + NX, NN)]
            x_copies += [
                send(other, ns.at[k + NX], nr.at[k + NX], x_peers[k]) for k in range(NX - 1)
            ]
            for copy in t_copies:
                copy.wait_recv()
            tz = [
                send(t_ref.at[z, :, c], tzs.at[k], tzr.at[k], z_peers[k]) for k in range(NZ - 1)
            ]
            sib_t = [send(t_ref.at[z, :, c], tss.at[0], tsr.at[0], sibling)]
            own[3].wait()
            two_ref[...] = twot_ref[...].T
        if s == 2:
            own[4].wait()
            w_ref[...] = wt_ref[...].T
    for k in (NZ - 1, 1, 2):
        at = lax.rem(z + k, NZ)
        bz[NZ - k - 1].wait_recv()
        sib_b.append(send(b_ref.at[at, :, c], bss.at[k], bsr.at[k], sibling))
        tz[NZ - k - 1].wait_recv()
        sib_t.append(send(t_ref.at[at, :, c], tss.at[k], tsr.at[k], sibling))

    for copy in z_copies + b_copies + t_copies + bz + tz + [across]:
        copy.wait_send()
    for copy in list(from_left.values()) + list(from_right.values()):
        copy.wait_send()
    for copy in to_sib + sib_b + sib_t + x_copies:
        copy.wait()


def gather(owners, slots, features, cotangent, wt, onet, twot):
    rows, tokens = features.shape
    cw, ct = cotangent.shape
    width, depth = wt.shape
    half = NY // 2
    pad = rows + rows // 3
    f32, bf16 = jnp.float32, jnp.bfloat16
    a, b, t, call, w, one, two = pl.pallas_call(
        gather_kernel,
        out_shape=(
            jax.ShapeDtypeStruct((NZ, NY, NC, pad, HEAD), bf16),
            jax.ShapeDtypeStruct((NZ, NY, NC, pad, KEEP - HEAD), bf16),
            jax.ShapeDtypeStruct((NZ, NY, NC, 8, 128), jnp.int32),
            jax.ShapeDtypeStruct((NN, cw, ct), bf16),
            jax.ShapeDtypeStruct((depth, width), bf16),
            jax.ShapeDtypeStruct((depth, width), f32),
            jax.ShapeDtypeStruct((depth, width), f32),
        ),
        in_specs=[VMEM] * 2 + [ANY] * 5,
        out_specs=(VMEM,) * 7,
        scratch_shapes=[
            pltpu.VMEM((rows, tokens), bf16),
            pltpu.VMEM((width, depth), bf16),
            pltpu.VMEM((width, depth), f32),
            pltpu.VMEM((width, depth), f32),
            DMA((NZ - 1,)), DMA((NZ - 1,)),
            DMA((half, NZ)), DMA((half, NZ)),
            DMA((half, NZ)), DMA((half, NZ)),
            DMA((NY + 1,)), DMA((NY + 1,)),
            DMA((NY - 1,)), DMA((NY - 1,)),
            DMA((NZ - 1,)), DMA((NZ - 1,)),
            DMA((NZ,)), DMA((NZ,)),
            DMA((NY - 1,)), DMA((NY - 1,)),
            DMA((NZ - 1,)), DMA((NZ - 1,)),
            DMA((NZ,)), DMA((NZ,)),
            DMA((NN - 1,)), DMA((NN - 1,)),
            DMA((5,)),
        ],
        compiler_params=pltpu.CompilerParams(
            collective_id=0, has_side_effects=True, vmem_limit_bytes=32 * 1024 * 1024
        ),
        name="gather_blocks",
    )(
        owners, slots,
        *(pltpu.with_memory_space_constraint(v, pltpu.HBM) for v in (features, cotangent, wt, onet, twot)),
    )
    many = NZ * NY * NC
    a, b, t = (v.reshape((many,) + v.shape[3:]) for v in (a, b, t))
    return a, b, t, call, w, one, two


def project_kernel(a_ref, b_ref, wt_ref, f_ref, own_ref, p1_ref, p2_ref, p3_ref):
    n = lax.axis_index("node")
    x, high = lax.rem(n, NX), n // NX
    blocks, pad, _ = a_ref.shape
    rows = pad * 3 // 4
    tokens = f_ref.shape[1] // NN
    extra = f_ref.shape[1] - KEEP

    def arrange(i, carry):
        at = pl.ds(pl.multiple_of(i * 4 * rows, 16), 4 * rows)
        a = a_ref[pl.ds(4 * i, 4)]
        b = b_ref[pl.ds(4 * i, 4)]
        f_ref[at, :HEAD] = jnp.concatenate([a[j, :rows] for j in range(4)], axis=0)
        f_ref[at, HEAD:KEEP] = jnp.concatenate([b[j, :rows] for j in range(4)], axis=0)
        ends = []
        for j in range(4):
            for k in range(HEAD // extra):
                ends.append(a[j, rows:, k * extra:(k + 1) * extra])
            ends.append(b[j, rows:])
        f_ref[at, KEEP:] = jnp.concatenate(ends, axis=0)
        return carry

    lax.fori_loop(0, blocks // 4, arrange, 0)

    for k, out in ((1, p1_ref), (2, p2_ref), (3, p3_ref), (0, own_ref)):
        for h in range(2):
            node = lax.rem(high + h, 2) * NX + lax.rem(x + k, NX)
            at = pl.ds(pl.multiple_of(node * tokens, tokens), tokens)
            out[h] = jnp.dot(wt_ref[...], f_ref[:, at], preferred_element_type=jnp.float32)


def project(a, b, wt):
    blocks, pad, _ = a.shape
    width, depth = wt.shape
    tokens = KEEP + (KEEP // 3)
    share = jax.ShapeDtypeStruct((2, width, tokens // NN), jnp.float32)
    return pl.pallas_call(
        project_kernel,
        out_shape=(jax.ShapeDtypeStruct((depth, tokens), jnp.bfloat16),) + (share,) * NX,
        in_specs=[VMEM] * 3,
        out_specs=(VMEM,) * (NX + 1),
        compiler_params=pltpu.CompilerParams(vmem_limit_bytes=32 * 1024 * 1024),
        name="arrange_and_project",
    )(a, b, wt)


def fixed_point(x):
    most = jnp.maximum(jnp.max(jnp.abs(x), axis=1, keepdims=True), LEAST)
    power = jnp.ceil(jnp.log2(most))
    q = jnp.round(x * (TOP * jnp.exp2(-power)))
    return jnp.clip(q, -TOP, TOP).astype(jnp.int32), power.astype(jnp.int32)


def code_of(x):
    a = jnp.abs(x)
    some = a >= 2.0**-126
    safe = jnp.where(some, a, 1.0)
    e = jnp.floor(jnp.log2(safe))
    code = jnp.round((e + 127.0) * 128.0 + (safe * jnp.exp2(-e) - 1.0) * 128.0)
    code = jnp.where(some, code, 0.0)
    return jnp.where(x < 0.0, -code, code).astype(jnp.int32)


def value_of(code):
    a = jnp.abs(code)
    e = lax.shift_right_logical(a, 7)
    m = lax.bitwise_and(a, 127)
    v = (1.0 + m.astype(jnp.float32) * (1.0 / 128.0)) * jnp.exp2(e.astype(jnp.float32) - 127.0)
    v = jnp.where(a == 0, 0.0, v)
    return jnp.where(code < 0, -v, v)


def exchange_kernel(
    tile_ref, f_ref, c_ref, w_ref, one_ref, two_ref, own_ref, p1_ref, p2_ref, p3_ref,
    inbox_ref, out_ref, grad, outbox, got, total, across_got,
    send_sem, recv_sem, xs, xr, acs, acr, loc,
):
    n = lax.axis_index("node")
    w = lax.axis_index("wide")
    many = outbox.shape[0]
    partner, x_peers = node_peers_of(n, w)
    width = w_ref.shape[2]
    full = width // 128 * 128
    rest = width - full

    def peer_of(i):
        step = lax.rem(i * 27, many)
        return lax.rem(w + step, many), step

    barrier = pltpu.get_barrier_semaphore()
    for peer in [partner] + x_peers:
        pl.semaphore_signal(barrier, inc=1, device_id=peer, device_id_type=MESH)

    def greet(i, carry):
        p, _ = peer_of(i)
        pl.semaphore_signal(barrier, inc=1, device_id=(n, p), device_id_type=MESH)
        return carry

    lax.fori_loop(1, many, greet, 0)

    part = grad.shape[0] // 3
    tokens = c_ref.shape[2]

    def multiply(i, carry):
        at = pl.ds(pl.multiple_of(i * part * TILE, 256), part * TILE)
        g = jnp.zeros((part * TILE, width), jnp.float32)
        for k in range(c_ref.shape[0]):
            g += lax.dot_general(
                f_ref[at, k * tokens:(k + 1) * tokens], c_ref[k],
                (((1,), (1,)), ((), ())), preferred_element_type=jnp.float32,
            )
        g = g.astype(jnp.bfloat16).astype(jnp.float32)
        grad[pl.ds(i * part, part)] = g.reshape(part, TILE, width)
        return carry

    lax.fori_loop(0, 3, multiply, 0)
    pl.semaphore_wait(barrier, many - 1 + NX)

    shares = (p1_ref, p2_ref, p3_ref)
    x_copies = []
    for k in range(NX - 1):
        copy = pltpu.make_async_remote_copy(
            src_ref=shares[k], dst_ref=got.at[k], send_sem=xs.at[k], recv_sem=xr.at[k],
            device_id=x_peers[k], device_id_type=MESH,
        )
        copy.start()
        x_copies.append(copy)

    def pack(p):
        b = tile_ref[p]
        g = grad[b]
        first = 0.9 * one_ref[b] + 0.1 * g
        second = 0.999 * two_ref[b] + 0.001 * g * g
        step = first * (rate / bias_one) / (jnp.sqrt(second * (1.0 / bias_two)) + 1e-08)
        weight = (w_ref[b].astype(jnp.float32) - step).astype(jnp.bfloat16)
        qf, pf = fixed_point(first)
        qs, ps = fixed_point(second)
        cw = code_of(weight.astype(jnp.float32))
        outbox[p, :, 0:full] = qf[:, :full].astype(jnp.int16)
        outbox[p, :, full:2 * full] = qs[:, :full].astype(jnp.int16)
        outbox[p, :, 2 * full:3 * full] = cw[:, :full].astype(jnp.int16)
        lane = lax.broadcasted_iota(jnp.int32, (TILE, 128 - 3 * rest), 1)
        powers = jnp.where(lane == 0, pf, ps)
        end = jnp.concatenate([qf[:, full:], qs[:, full:], cw[:, full:], powers], axis=1)
        outbox[p, :, 3 * full:] = end.astype(jnp.int16)

    def copy_to(p, step):
        return pltpu.make_async_remote_copy(
            src_ref=outbox.at[p], dst_ref=inbox_ref.at[w],
            send_sem=send_sem.at[step], recv_sem=recv_sem.at[step],
            device_id=(n, p), device_id_type=MESH,
        )

    def send(i, carry):
        p, step = peer_of(i)
        pack(p)
        copy_to(p, step).start()
        return carry

    lax.fori_loop(1, many, send, 0)
    pack(w)
    mine = pltpu.make_async_copy(outbox.at[w], inbox_ref.at[w], loc)
    mine.start()

    for copy in x_copies:
        copy.wait_recv()
    total[...] = own_ref[1] + got[0, 1] + got[1, 1] + got[2, 1]
    across = pltpu.make_async_remote_copy(
        src_ref=total, dst_ref=across_got, send_sem=acs, recv_sem=acr,
        device_id=partner, device_id_type=MESH,
    )
    across.start()
    near = own_ref[0] + got[0, 0] + got[1, 0] + got[2, 0]
    across.wait_recv()
    out_ref[...] = (near + across_got[...]).astype(jnp.bfloat16)

    def finish(i, carry):
        p, step = peer_of(i)
        copy_to(p, step).wait()
        return carry

    lax.fori_loop(1, many, finish, 0)
    mine.wait()
    across.wait_send()
    for copy in x_copies:
        copy.wait_send()


def exchange(tile_of, rows, cots, weight, one, two, shares, peers):
    depth, width = weight.shape
    lanes = 3 * (width // 128 * 128) + 128
    blocks = depth // TILE
    share = shares[0].shape
    f32 = jnp.float32
    weight, one, two = (v.reshape(blocks, TILE, width) for v in (weight, one, two))
    return pl.pallas_call(
        exchange_kernel,
        out_shape=(
            pltpu.HBM((peers, TILE, lanes), jnp.int16),
            jax.ShapeDtypeStruct(share[1:], jnp.bfloat16),
        ),
        in_specs=[SMEM] + [VMEM] * 9,
        out_specs=(HBM, VMEM),
        scratch_shapes=[
            pltpu.VMEM((blocks, TILE, width), f32),
            pltpu.VMEM((peers, TILE, lanes), jnp.int16),
            pltpu.VMEM((NX - 1,) + share, f32),
            pltpu.VMEM(share[1:], f32),
            pltpu.VMEM(share[1:], f32),
            DMA((peers,)), DMA((peers,)),
            DMA((NX - 1,)), DMA((NX - 1,)),
            DMA, DMA, DMA,
        ],
        compiler_params=pltpu.CompilerParams(
            collective_id=1, has_side_effects=True, vmem_limit_bytes=32 * 1024 * 1024
        ),
        name="update_and_exchange",
    )(tile_of, rows, cots, weight, one, two, *shares)


PER = 4


def place_kernel(from_ref, inbox_ref, weight_ref, first_ref, second_ref, held, sems):
    width = weight_ref.shape[3]
    capacity = held.shape[0]
    full = width // 128 * 128
    rest = width - full
    step = pl.program_id(0)

    def fetch(s):
        at = jnp.maximum(from_ref[s], 0)
        return pltpu.make_async_copy(inbox_ref.at[at], held.at[s], sems.at[s])

    @pl.when(step == 0)
    def _():
        def start(s, carry):
            fetch(s).start()
            return carry

        lax.fori_loop(0, capacity, start, 0)

    for j in range(PER):
        s = step * PER + j
        fetch(s).wait()

        @pl.when(from_ref[s] >= 0)
        def _():
            q = held[s].astype(jnp.int32)
            end = q[:, 3 * full:]
            pf = jnp.exp2(end[:, 3 * rest:3 * rest + 1].astype(jnp.float32)) * (1.0 / TOP)
            ps = jnp.exp2(end[:, 3 * rest + 1:3 * rest + 2].astype(jnp.float32)) * (1.0 / TOP)
            first_ref[0, j, :, :full] = q[:, :full].astype(jnp.float32) * pf
            first_ref[0, j, :, full:] = end[:, :rest].astype(jnp.float32) * pf
            second_ref[0, j, :, :full] = q[:, full:2 * full].astype(jnp.float32) * ps
            second_ref[0, j, :, full:] = end[:, rest:2 * rest].astype(jnp.float32) * ps
            weight_ref[0, j, :, :full] = value_of(q[:, 2 * full:3 * full]).astype(jnp.bfloat16)
            weight_ref[0, j, :, full:] = value_of(end[:, 2 * rest:3 * rest]).astype(jnp.bfloat16)

        @pl.when(from_ref[s] < 0)
        def _():
            for ref in (weight_ref, first_ref, second_ref):
                ref[0, j] = jnp.zeros(ref.shape[2:], ref.dtype)


def place(source, inbox, capacity, width):
    shape = (1, capacity, TILE, width)
    block = pl.BlockSpec((1, PER, TILE, width), lambda i: (0, i, 0, 0))
    return pl.pallas_call(
        place_kernel,
        out_shape=(
            jax.ShapeDtypeStruct(shape, jnp.bfloat16),
            jax.ShapeDtypeStruct(shape, jnp.float32),
            jax.ShapeDtypeStruct(shape, jnp.float32),
        ),
        grid=(capacity // PER,),
        in_specs=[SMEM, HBM],
        out_specs=(block,) * 3,
        scratch_shapes=[
            pltpu.VMEM((capacity,) + inbox.shape[1:], jnp.int16),
            DMA((capacity,)),
        ],
        compiler_params=pltpu.CompilerParams(vmem_limit_bytes=32 * 1024 * 1024),
        name="place_tiles",
    )(source, pltpu.with_memory_space_constraint(inbox, pltpu.HBM))


def on_device(features, weight, moment_one, moment_two, cotangent, new_owner, new_slot):
    peers = lax.axis_size("wide")
    owners = new_owner.reshape(-1)
    blocks = owners.shape[0]
    capacity = blocks + blocks // 6
    width = weight.shape[1]
    a, b, tables, cots, weight_rows, one, two = gather(
        new_owner[0], new_slot[0], features, cotangent.T, weight.T, moment_one.T, moment_two.T
    )
    rows, *shares = project(a, b, weight.T)
    every = lax.broadcasted_iota(jnp.int32, (blocks, peers), 1)
    index = lax.broadcasted_iota(jnp.int32, (blocks, peers), 0)
    tile_of = jnp.sum(jnp.where(owners[:, None] == every, index, 0), axis=0)
    inbox, total = exchange(tile_of, rows, cots, weight_rows, one, two, shares, peers)
    mine = tables[:, 0, :blocks] == lax.axis_index("wide")
    dest = jnp.min(jnp.where(mine, tables[:, 1, :blocks], capacity), axis=1)
    slot = lax.broadcasted_iota(jnp.int32, (peers, capacity), 1)
    source = lax.broadcasted_iota(jnp.int32, (peers, capacity), 0)
    source = jnp.max(jnp.where(dest[:, None] == slot, source, -1), axis=0)
    moved = place(source, inbox, capacity, width)
    return (total.T,) + tuple(moved)


def solution(mesh):
    placed = (
        P(("node", "wide"), None),
        P("node", "wide"),
        P("node", "wide"),
        P("node", "wide"),
        P("node", "wide"),
        P("node", "wide", None),
        P("node", "wide", None),
    )
    return jax.shard_map(
        on_device,
        mesh=mesh,
        in_specs=placed,
        out_specs=(
            P("node", "wide"),
            P("node", "wide", None, None),
            P("node", "wide", None, None),
            P("node", "wide", None, None),
        ),
        check_vma=False,
    )
```

```python
import jax
import jax.numpy as jnp
from jax import lax
from jax.experimental import pallas as pl
from jax.experimental.pallas import tpu as pltpu
from jax.sharding import PartitionSpec as P

TILE = 32
NZ, NY, NC = 4, 8, 2
NX = 4
NN = 2 * NX
MESH = pl.DeviceIdType.MESH
ANY = pl.BlockSpec(memory_space=pl.ANY)
HBM = pl.BlockSpec(memory_space=pltpu.HBM)
VMEM = pl.BlockSpec(memory_space=pltpu.VMEM)
SMEM = pl.BlockSpec(memory_space=pltpu.SMEM)
DMA = pltpu.SemaphoreType.DMA

rate = 0.02
bias_one = 1.0 - 0.9**10
bias_two = 1.0 - 0.999**10

TOP = 32767.0
LEAST = 2.0**-100


def place_of(w):
    return w // (NY * NC), (w // NC) % NY, w % NC


def node_peers_of(n, w):
    x = lax.rem(n, NX)
    base = n - x
    return (lax.rem(n + NX, NN), w), [(base + lax.rem(x + k, NX), w) for k in range(1, NX)]


HEAD = 1024
AHEAD = 9
KEEP = 1536


def gather_kernel(
    owner_in, slot_in, x_in, c_in, wt_in, onet_in, twot_in,
    a_ref, b_ref, t_ref, tile_ref, call_ref, w_ref, one_ref, two_ref,
    owner_ref, slot_ref, x_ref, wt_ref, onet_ref, twot_ref,
    zs, zr, rs, rr, ls, lr, ss, sr, bs, br, bzs, bzr, bss, bsr,
    ts, tr, tzs, tzr, tss, tsr, ns, nr, loc,
):
    n = lax.axis_index("node")
    w = lax.axis_index("wide")
    z, y, c = place_of(w)

    def wide(zz, yy, cc):
        return (n, (lax.rem(zz + NZ, NZ) * NY + lax.rem(yy + NY, NY)) * NC + cc)

    sibling = wide(z, y, 1 - c)
    y_peers = [wide(z, y + k, c) for k in range(1, NY)]
    right, left = y_peers[0], y_peers[-1]
    z_peers = [wide(z + k, y, c) for k in range(1, NZ)]
    partner, x_peers = node_peers_of(n, w)

    barrier = pltpu.get_barrier_semaphore()
    peers = [sibling, partner] + y_peers + z_peers + x_peers
    for peer in peers:
        pl.semaphore_signal(barrier, inc=1, device_id=peer, device_id_type=MESH)

    own = [
        pltpu.make_async_copy(src, dst, loc.at[i])
        for i, (src, dst) in enumerate((
            (x_in, x_ref), (c_in, call_ref.at[n]),
            (onet_in, onet_ref), (twot_in, twot_ref), (wt_in, wt_ref),
            (owner_in, owner_ref), (slot_in, slot_ref),
        ))
    ]
    for copy in own:
        copy.start()
    own[0].wait()

    rows = x_ref.shape[0]
    extra = (x_ref.shape[1] - KEEP)
    a_ref[z, y, c, :rows, :] = x_ref[:, :HEAD]
    b_ref[z, y, c, :rows, :] = x_ref[:, HEAD:KEEP]
    for k in range(HEAD // extra):
        a_ref[z, y, c, rows:, k * extra:(k + 1) * extra] = x_ref[4 * k:4 * k + 4, KEEP:]
    b_ref[z, y, c, rows:, :] = x_ref[rows - 4:, KEEP:]
    own[5].wait()
    own[6].wait()
    t_ref[z, y, c, 0:1, :owner_ref.shape[1]] = owner_ref[...]
    t_ref[z, y, c, 1:2, :slot_ref.shape[1]] = slot_ref[...]
    own[1].wait()

    pl.semaphore_wait(barrier, len(peers))

    def send(ref, s, r, peer):
        copy = pltpu.make_async_remote_copy(
            src_ref=ref, dst_ref=ref, send_sem=s, recv_sem=r,
            device_id=peer, device_id_type=MESH,
        )
        copy.start()
        return copy

    b_copies = [
        send(b_ref.at[z, y, c], bs.at[k], br.at[k], y_peers[k]) for k in range(NY - 1)
    ]
    z_copies = [
        send(a_ref.at[z, y, c], zs.at[k], zr.at[k], z_peers[k]) for k in range(NZ - 1)
    ]
    across = send(call_ref.at[n], ns.at[0], nr.at[0], partner)
    x_copies = [
        send(call_ref.at[n], ns.at[k + 1], nr.at[k + 1], x_peers[k]) for k in range(NX - 1)
    ]
    t_copies = [
        send(t_ref.at[z, y, c], ts.at[k], tr.at[k], y_peers[k]) for k in range(NY - 1)
    ]

    def block(k, yy):
        return a_ref.at[lax.rem(z + k, NZ), lax.rem(yy + NY, NY), c]

    half = NY // 2
    order = (0, NZ - 1, 1, 2)
    from_left, from_right, to_sib = {}, {}, []
    for s in range(half + 1):
        for i, k in enumerate(order):
            if s == 0:
                if k > 0:
                    z_copies[NZ - k - 1].wait_recv()
            else:
                if (s - 1, k) in from_left:
                    from_left[s - 1, k].wait_recv()
                if (s - 1, k) in from_right:
                    from_right[s - 1, k].wait_recv()
            if s < half:
                last = s == half - 1
                if not last or i % 2 == 0:
                    from_left[s, k] = send(block(k, y - s), rs.at[s, k], rr.at[s, k], right)
                if not last or i % 2 == 1:
                    from_right[s, k] = send(block(k, y + s), ls.at[s, k], lr.at[s, k], left)
            if s == 0 and k == 0:
                for copy in b_copies:
                    copy.wait_recv()
                bz = [
                    send(b_ref.at[z, :, c], bzs.at[j], bzr.at[j], z_peers[j])
                    for j in range(NZ - 1)
                ]
        to_sib.append(send(a_ref.at[:, lax.rem(y - s + NY, NY), c], ss.at[2 * s], sr.at[2 * s], sibling))
        if 0 < s < half:
            to_sib.append(
                send(a_ref.at[:, lax.rem(y + s, NY), c], ss.at[2 * s - 1], sr.at[2 * s - 1], sibling)
            )
        if s == 0:
            sib_b = [send(b_ref.at[z, :, c], bss.at[0], bsr.at[0], sibling)]
            lane = lax.broadcasted_iota(jnp.int32, tile_ref.shape, 1)
            tile = jnp.zeros(tile_ref.shape, jnp.int32)
            for t in range(owner_ref.shape[1]):
                tile = jnp.where(lane == owner_ref[0:1, t:t + 1], t, tile)
            tile_ref[...] = tile
            own[2].wait()
            one_ref[...] = onet_ref[...].T
        if s == 1:
            across.wait_recv()
            other = call_ref.at[lax.rem(n + NX, NN)]
            x_copies += [
                send(other, ns.at[k + NX], nr.at[k + NX], x_peers[k]) for k in range(NX - 1)
            ]
            for copy in t_copies:
                copy.wait_recv()
            tz = [
                send(t_ref.at[z, :, c], tzs.at[k], tzr.at[k], z_peers[k]) for k in range(NZ - 1)
            ]
            sib_t = [send(t_ref.at[z, :, c], tss.at[0], tsr.at[0], sibling)]
            own[3].wait()
            two_ref[...] = twot_ref[...].T
        if s == 2:
            own[4].wait()
            w_ref[...] = wt_ref[...].T
    for k in (NZ - 1, 1, 2):
        at = lax.rem(z + k, NZ)
        bz[NZ - k - 1].wait_recv()
        sib_b.append(send(b_ref.at[at, :, c], bss.at[k], bsr.at[k], sibling))
        tz[NZ - k - 1].wait_recv()
        sib_t.append(send(t_ref.at[at, :, c], tss.at[k], tsr.at[k], sibling))

    for copy in z_copies + b_copies + t_copies + bz + tz + [across]:
        copy.wait_send()
    for copy in list(from_left.values()) + list(from_right.values()):
        copy.wait_send()
    for copy in to_sib + sib_b + sib_t + x_copies:
        copy.wait()


def gather(owners, slots, features, cotangent, wt, onet, twot):
    rows, tokens = features.shape
    cw, ct = cotangent.shape
    width, depth = wt.shape
    half = NY // 2
    pad = rows + rows // 3
    f32, bf16 = jnp.float32, jnp.bfloat16
    a, b, t, tile, call, w, one, two = pl.pallas_call(
        gather_kernel,
        out_shape=(
            jax.ShapeDtypeStruct((NZ, NY, NC, pad, HEAD), bf16),
            jax.ShapeDtypeStruct((NZ, NY, NC, pad, KEEP - HEAD), bf16),
            jax.ShapeDtypeStruct((NZ, NY, NC, 8, 128), jnp.int32),
            jax.ShapeDtypeStruct((1, 128), jnp.int32),
            jax.ShapeDtypeStruct((NN, cw, ct), bf16),
            jax.ShapeDtypeStruct((depth, width), bf16),
            jax.ShapeDtypeStruct((depth, width), f32),
            jax.ShapeDtypeStruct((depth, width), f32),
        ),
        in_specs=[HBM] * 7,
        out_specs=(VMEM,) * 8,
        scratch_shapes=[
            pltpu.VMEM(owners.shape, jnp.int32),
            pltpu.VMEM(slots.shape, jnp.int32),
            pltpu.VMEM((rows, tokens), bf16),
            pltpu.VMEM((width, depth), bf16),
            pltpu.VMEM((width, depth), f32),
            pltpu.VMEM((width, depth), f32),
            DMA((NZ - 1,)), DMA((NZ - 1,)),
            DMA((half, NZ)), DMA((half, NZ)),
            DMA((half, NZ)), DMA((half, NZ)),
            DMA((NY + 1,)), DMA((NY + 1,)),
            DMA((NY - 1,)), DMA((NY - 1,)),
            DMA((NZ - 1,)), DMA((NZ - 1,)),
            DMA((NZ,)), DMA((NZ,)),
            DMA((NY - 1,)), DMA((NY - 1,)),
            DMA((NZ - 1,)), DMA((NZ - 1,)),
            DMA((NZ,)), DMA((NZ,)),
            DMA((NN - 1,)), DMA((NN - 1,)),
            DMA((7,)),
        ],
        compiler_params=pltpu.CompilerParams(
            collective_id=0, has_side_effects=True, vmem_limit_bytes=32 * 1024 * 1024
        ),
        name="gather_blocks",
    )(*(
        pltpu.with_memory_space_constraint(v, pltpu.HBM)
        for v in (owners, slots, features, cotangent, wt, onet, twot)
    ))
    many = NZ * NY * NC
    a, b, t = (v.reshape((many,) + v.shape[3:]) for v in (a, b, t))
    return a, b, t, tile, call, w, one, two


def arrange(a_ref, b_ref, f_ref):
    blocks, pad, _ = a_ref.shape
    rows = pad * 3 // 4
    extra = f_ref.shape[1] - KEEP

    def four(i, carry):
        at = pl.ds(pl.multiple_of(i * 4 * rows, 16), 4 * rows)
        a = a_ref[pl.ds(4 * i, 4)]
        b = b_ref[pl.ds(4 * i, 4)]
        f_ref[at, :HEAD] = jnp.concatenate([a[j, :rows] for j in range(4)], axis=0)
        f_ref[at, HEAD:KEEP] = jnp.concatenate([b[j, :rows] for j in range(4)], axis=0)
        ends = []
        for j in range(4):
            for k in range(HEAD // extra):
                ends.append(a[j, rows:, k * extra:(k + 1) * extra])
            ends.append(b[j, rows:])
        f_ref[at, KEEP:] = jnp.concatenate(ends, axis=0)
        return carry

    lax.fori_loop(0, blocks // 4, four, 0)


def fixed_point(x):
    most = jnp.maximum(jnp.max(jnp.abs(x), axis=1, keepdims=True), LEAST)
    power = jnp.ceil(jnp.log2(most))
    q = jnp.round(x * (TOP * jnp.exp2(-power)))
    return jnp.clip(q, -TOP, TOP).astype(jnp.int32), power.astype(jnp.int32)


def code_of(x):
    a = jnp.abs(x)
    some = a >= 2.0**-126
    safe = jnp.where(some, a, 1.0)
    e = jnp.floor(jnp.log2(safe))
    code = jnp.round((e + 127.0) * 128.0 + (safe * jnp.exp2(-e) - 1.0) * 128.0)
    code = jnp.where(some, code, 0.0)
    return jnp.where(x < 0.0, -code, code).astype(jnp.int32)


def value_of(code):
    a = jnp.abs(code)
    e = lax.shift_right_logical(a, 7)
    m = lax.bitwise_and(a, 127)
    v = (1.0 + m.astype(jnp.float32) * (1.0 / 128.0)) * jnp.exp2(e.astype(jnp.float32) - 127.0)
    v = jnp.where(a == 0, 0.0, v)
    return jnp.where(code < 0, -v, v)


def exchange_kernel(
    tile_ref, a_ref, b_ref, t_ref, c_ref, wt_ref, w_ref, one_ref, two_ref,
    inbox_ref, out_ref, from_ref, f_ref, grad, outbox, share, got, total, across_got,
    send_sem, recv_sem, xs, xr, acs, acr, loc,
):
    n = lax.axis_index("node")
    w = lax.axis_index("wide")
    many = outbox.shape[0]
    partner, x_peers = node_peers_of(n, w)
    width = w_ref.shape[2]
    full = width // 128 * 128
    rest = width - full

    z, y, c = place_of(w)
    x, high = lax.rem(n, NX), n // NX

    def peer_of(i):
        step = lax.rem(i * 27, many)
        sign = 1 - 2 * c
        dz, dy, dc = place_of(step)
        to_z = lax.rem(z + NZ + sign * dz, NZ)
        to_y = lax.rem(y + NY + sign * dy, NY)
        return (to_z * NY + to_y) * NC + lax.rem(c + dc, NC), step

    barrier = pltpu.get_barrier_semaphore()
    for peer in [partner] + x_peers:
        pl.semaphore_signal(barrier, inc=1, device_id=peer, device_id_type=MESH)

    def greet(i, carry):
        p, _ = peer_of(i)
        pl.semaphore_signal(barrier, inc=1, device_id=(n, p), device_id_type=MESH)
        return carry

    lax.fori_loop(1, many, greet, 0)

    arrange(a_ref, b_ref, f_ref)
    part = grad.shape[0] // 3
    tokens = c_ref.shape[2]

    def multiply(i, carry):
        at = pl.ds(pl.multiple_of(i * part * TILE, 256), part * TILE)
        g = jnp.zeros((part * TILE, width), jnp.float32)
        for k in range(c_ref.shape[0]):
            g += lax.dot_general(
                f_ref[at, k * tokens:(k + 1) * tokens], c_ref[k],
                (((1,), (1,)), ((), ())), preferred_element_type=jnp.float32,
            )
        g = g.astype(jnp.bfloat16).astype(jnp.float32)
        grad[pl.ds(i * part, part)] = g.reshape(part, TILE, width)
        return carry

    lax.fori_loop(0, 3, multiply, 0)
    pl.semaphore_wait(barrier, many - 1 + NX)

    def pack(p):
        b = tile_ref[0, p]
        g = grad[b]
        first = 0.9 * one_ref[b] + 0.1 * g
        second = 0.999 * two_ref[b] + 0.001 * g * g
        step = first * (rate / bias_one) / (jnp.sqrt(second * (1.0 / bias_two)) + 1e-08)
        weight = (w_ref[b].astype(jnp.float32) - step).astype(jnp.bfloat16)
        qf, pf = fixed_point(first)
        qs, ps = fixed_point(second)
        cw = code_of(weight.astype(jnp.float32))
        outbox[p, :, 0:full] = qf[:, :full].astype(jnp.int16)
        outbox[p, :, full:2 * full] = qs[:, :full].astype(jnp.int16)
        outbox[p, :, 2 * full:3 * full] = cw[:, :full].astype(jnp.int16)
        lane = lax.broadcasted_iota(jnp.int32, (TILE, 128 - 3 * rest), 1)
        powers = jnp.where(lane == 0, pf, ps)
        end = jnp.concatenate([qf[:, full:], qs[:, full:], cw[:, full:], powers], axis=1)
        outbox[p, :, 3 * full:] = end.astype(jnp.int16)

    def copy_to(p, step):
        return pltpu.make_async_remote_copy(
            src_ref=outbox.at[p], dst_ref=inbox_ref.at[w],
            send_sem=send_sem.at[step], recv_sem=recv_sem.at[step],
            device_id=(n, p), device_id_type=MESH,
        )

    def send(i, carry):
        p, step = peer_of(i)
        pack(p)
        copy_to(p, step).start()
        return carry

    lax.fori_loop(1, AHEAD, send, 0)

    def partial(k, half):
        node = lax.rem(high + half, 2) * NX + lax.rem(x + k, NX)
        at = pl.ds(pl.multiple_of(node * tokens, tokens), tokens)
        share[k, half] = jnp.dot(wt_ref[...], f_ref[:, at], preferred_element_type=jnp.float32)

    x_copies = []
    for k in range(1, NX):
        for half in range(2):
            partial(k, half)
        copy = pltpu.make_async_remote_copy(
            src_ref=share.at[k], dst_ref=got.at[k - 1],
            send_sem=xs.at[k - 1], recv_sem=xr.at[k - 1],
            device_id=x_peers[k - 1], device_id_type=MESH,
        )
        copy.start()
        x_copies.append(copy)
    lax.fori_loop(AHEAD, many, send, 0)
    for half in range(2):
        partial(0, half)
    pack(w)
    mine = pltpu.make_async_copy(outbox.at[w], inbox_ref.at[w], loc)
    mine.start()

    blocks = grad.shape[0]
    lane = lax.broadcasted_iota(jnp.int32, (many, 128), 1)
    ours = jnp.logical_and(t_ref[:, 0, :] == w, lane < blocks)
    slot = jnp.min(jnp.where(ours, t_ref[:, 1, :], 128), axis=1, keepdims=True)
    source = lax.broadcasted_iota(jnp.int32, (many, 128), 0)
    from_ref[...] = jnp.max(jnp.where(slot == lane, source, -1), axis=0, keepdims=True)

    for copy in x_copies:
        copy.wait_recv()
    total[...] = share[0, 1] + got[0, 1] + got[1, 1] + got[2, 1]
    across = pltpu.make_async_remote_copy(
        src_ref=total, dst_ref=across_got, send_sem=acs, recv_sem=acr,
        device_id=partner, device_id_type=MESH,
    )
    across.start()
    near = share[0, 0] + got[0, 0] + got[1, 0] + got[2, 0]
    across.wait_recv()
    out_ref[...] = (near + across_got[...]).astype(jnp.bfloat16)

    def finish(i, carry):
        p, step = peer_of(i)
        copy_to(p, step).wait()
        return carry

    lax.fori_loop(1, many, finish, 0)
    mine.wait()
    across.wait_send()
    for copy in x_copies:
        copy.wait_send()


def exchange(tile_of, a, b, tables, cots, wt, weight, one, two):
    depth, width = weight.shape
    lanes = 3 * (width // 128 * 128) + 128
    blocks = depth // TILE
    peers = tables.shape[0]
    tokens = cots.shape[2]
    f32 = jnp.float32
    weight, one, two = (v.reshape(blocks, TILE, width) for v in (weight, one, two))
    return pl.pallas_call(
        exchange_kernel,
        out_shape=(
            pltpu.HBM((peers, TILE, lanes), jnp.int16),
            jax.ShapeDtypeStruct((width, tokens), jnp.bfloat16),
            jax.ShapeDtypeStruct((1, 128), jnp.int32),
        ),
        in_specs=[SMEM] + [VMEM] * 8,
        out_specs=(HBM, VMEM, VMEM),
        scratch_shapes=[
            pltpu.VMEM((depth, tokens * NN), jnp.bfloat16),
            pltpu.VMEM((blocks, TILE, width), f32),
            pltpu.VMEM((peers, TILE, lanes), jnp.int16),
            pltpu.VMEM((NX, 2, width, tokens), f32),
            pltpu.VMEM((NX - 1, 2, width, tokens), f32),
            pltpu.VMEM((width, tokens), f32),
            pltpu.VMEM((width, tokens), f32),
            DMA((peers,)), DMA((peers,)),
            DMA((NX - 1,)), DMA((NX - 1,)),
            DMA, DMA, DMA,
        ],
        compiler_params=pltpu.CompilerParams(
            collective_id=1, has_side_effects=True, vmem_limit_bytes=32 * 1024 * 1024
        ),
        name="update_and_exchange",
    )(tile_of, a, b, tables, cots, wt, weight, one, two)


PER = 7


def place_kernel(
    from_ref, inbox_ref, total_ref, weight_ref, first_ref, second_ref, out_ref, held, sems
):
    width = weight_ref.shape[3]
    capacity = held.shape[0]
    full = width // 128 * 128
    rest = width - full
    step = pl.program_id(0)

    def fetch(s):
        at = jnp.maximum(from_ref[0, s], 0)
        return pltpu.make_async_copy(inbox_ref.at[at], held.at[s], sems.at[s])

    @pl.when(step == 0)
    def _():
        def start(s, carry):
            fetch(s).start()
            return carry

        lax.fori_loop(0, capacity, start, 0)
        out_ref[...] = total_ref[...]

    for j in range(PER):
        s = step * PER + j
        fetch(s).wait()
        some = from_ref[0, s] >= 0
        q = jnp.where(some, held[s].astype(jnp.int32), 0)
        end = q[:, 3 * full:]
        pf = jnp.exp2(end[:, 3 * rest:3 * rest + 1].astype(jnp.float32)) * (1.0 / TOP)
        ps = jnp.exp2(end[:, 3 * rest + 1:3 * rest + 2].astype(jnp.float32)) * (1.0 / TOP)
        first_ref[0, j, :, :full] = q[:, :full].astype(jnp.float32) * pf
        first_ref[0, j, :, full:] = end[:, :rest].astype(jnp.float32) * pf
        second_ref[0, j, :, :full] = q[:, full:2 * full].astype(jnp.float32) * ps
        second_ref[0, j, :, full:] = end[:, rest:2 * rest].astype(jnp.float32) * ps
        weight_ref[0, j, :, :full] = value_of(q[:, 2 * full:3 * full]).astype(jnp.bfloat16)
        weight_ref[0, j, :, full:] = value_of(end[:, 2 * rest:3 * rest]).astype(jnp.bfloat16)


def place(source, inbox, total, capacity):
    shape = (1, capacity, TILE, total.shape[0])
    block = pl.BlockSpec((1, PER) + shape[2:], lambda i: (0, i, 0, 0))
    whole = pl.BlockSpec(total.shape, lambda i: (0, 0))
    return pl.pallas_call(
        place_kernel,
        out_shape=(
            jax.ShapeDtypeStruct(shape, jnp.bfloat16),
            jax.ShapeDtypeStruct(shape, jnp.float32),
            jax.ShapeDtypeStruct(shape, jnp.float32),
            jax.ShapeDtypeStruct(total.shape, total.dtype),
        ),
        grid=(capacity // PER,),
        in_specs=[SMEM, HBM, whole],
        out_specs=(block,) * 3 + (whole,),
        scratch_shapes=[
            pltpu.VMEM((capacity,) + inbox.shape[1:], jnp.int16),
            DMA((capacity,)),
        ],
        compiler_params=pltpu.CompilerParams(vmem_limit_bytes=32 * 1024 * 1024),
        name="place_tiles",
    )(source, pltpu.with_memory_space_constraint(inbox, pltpu.HBM), total)


def on_device(features, weight, moment_one, moment_two, cotangent, new_owner, new_slot):
    blocks = new_owner.shape[2]
    capacity = blocks + blocks // 6
    wt = weight.T
    a, b, tables, tile_of, cots, weight_rows, one, two = gather(
        new_owner[0], new_slot[0], features, cotangent.T, wt, moment_one.T, moment_two.T
    )
    inbox, total, source = exchange(tile_of, a, b, tables, cots, wt, weight_rows, one, two)
    *moved, projected = place(source, inbox, total, capacity)
    return (projected.T,) + tuple(moved)


def solution(mesh):
    placed = (
        P(("node", "wide"), None),
        P("node", "wide"),
        P("node", "wide"),
        P("node", "wide"),
        P("node", "wide"),
        P("node", "wide", None),
        P("node", "wide", None),
    )
    return jax.shard_map(
        on_device,
        mesh=mesh,
        in_specs=placed,
        out_specs=(
            P("node", "wide"),
            P("node", "wide", None, None),
            P("node", "wide", None, None),
            P("node", "wide", None, None),
        ),
        check_vma=False,
    )
```

```python
import jax
import jax.numpy as jnp
from jax import lax
from jax.experimental import pallas as pl
from jax.experimental.pallas import tpu as pltpu
from jax.sharding import PartitionSpec as P

TILE = 32
NZ, NY, NC = 4, 8, 2
NX = 4
NN = 2 * NX
MESH = pl.DeviceIdType.MESH
ANY = pl.BlockSpec(memory_space=pl.ANY)
HBM = pl.BlockSpec(memory_space=pltpu.HBM)
VMEM = pl.BlockSpec(memory_space=pltpu.VMEM)
SMEM = pl.BlockSpec(memory_space=pltpu.SMEM)
DMA = pltpu.SemaphoreType.DMA

rate = 0.02
bias_one = 1.0 - 0.9**10
bias_two = 1.0 - 0.999**10

TOP = 32767.0
LEAST = 2.0**-100


def place_of(w):
    return w // (NY * NC), (w // NC) % NY, w % NC


def node_peers_of(n, w):
    x = lax.rem(n, NX)
    base = n - x
    return (lax.rem(n + NX, NN), w), [(base + lax.rem(x + k, NX), w) for k in range(1, NX)]


HEAD = 1280
AHEAD = 9
KEEP = 1536


def gather_kernel(
    owner_in, slot_in, x_in, c_in, wt_in, onet_in, twot_in,
    a_ref, b_ref, t_ref, tile_ref, call_ref, w_ref, one_ref, two_ref,
    owner_ref, slot_ref, x_ref, wt_ref, onet_ref, twot_ref,
    zs, zr, rs, rr, ls, lr, ss, sr, bs, br, bzs, bzr, bss, bsr,
    ts, tr, tzs, tzr, tss, tsr, ns, nr, loc,
):
    n = lax.axis_index("node")
    w = lax.axis_index("wide")
    z, y, c = place_of(w)

    def wide(zz, yy, cc):
        return (n, (lax.rem(zz + NZ, NZ) * NY + lax.rem(yy + NY, NY)) * NC + cc)

    sibling = wide(z, y, 1 - c)
    y_peers = [wide(z, y + k, c) for k in range(1, NY)]
    right, left = y_peers[0], y_peers[-1]
    z_peers = [wide(z + k, y, c) for k in range(1, NZ)]
    partner, x_peers = node_peers_of(n, w)

    barrier = pltpu.get_barrier_semaphore()
    peers = [sibling, partner] + y_peers + z_peers + x_peers
    for peer in peers:
        pl.semaphore_signal(barrier, inc=1, device_id=peer, device_id_type=MESH)

    own = [
        pltpu.make_async_copy(src, dst, loc.at[i])
        for i, (src, dst) in enumerate((
            (x_in, x_ref), (c_in, call_ref.at[n]),
            (onet_in, onet_ref), (twot_in, twot_ref), (wt_in, wt_ref),
            (owner_in, owner_ref), (slot_in, slot_ref),
        ))
    ]
    for copy in own:
        copy.start()
    own[0].wait()

    rows = x_ref.shape[0]
    extra = x_ref.shape[1] - KEEP
    third = HEAD - 2 * extra
    a_ref[z, y, c, :rows, :] = x_ref[:, :HEAD]
    b_ref[z, y, c, :rows, :] = x_ref[:, HEAD:KEEP]
    for k in range(2):
        a_ref[z, y, c, rows:, k * extra:(k + 1) * extra] = x_ref[4 * k:4 * k + 4, KEEP:]
    a_ref[z, y, c, rows:, 2 * extra:] = x_ref[rows - 4:, KEEP:KEEP + third]
    b_ref[z, y, c, rows:, :] = x_ref[rows - 4:, KEEP + third:]
    own[5].wait()
    own[6].wait()
    t_ref[z, y, c, 0:1, :owner_ref.shape[1]] = owner_ref[...]
    t_ref[z, y, c, 1:2, :slot_ref.shape[1]] = slot_ref[...]
    own[1].wait()

    pl.semaphore_wait(barrier, len(peers))

    def send(ref, s, r, peer):
        copy = pltpu.make_async_remote_copy(
            src_ref=ref, dst_ref=ref, send_sem=s, recv_sem=r,
            device_id=peer, device_id_type=MESH,
        )
        copy.start()
        return copy

    b_copies = [
        send(b_ref.at[z, y, c], bs.at[k], br.at[k], y_peers[k]) for k in range(NY - 1)
    ]
    z_copies = [
        send(a_ref.at[z, y, c], zs.at[k], zr.at[k], z_peers[k]) for k in range(NZ - 1)
    ]
    across = send(call_ref.at[n], ns.at[0], nr.at[0], partner)
    x_copies = [
        send(call_ref.at[n], ns.at[k + 1], nr.at[k + 1], x_peers[k]) for k in range(NX - 1)
    ]
    t_copies = [
        send(t_ref.at[z, y, c], ts.at[k], tr.at[k], y_peers[k]) for k in range(NY - 1)
    ]

    def block(k, yy):
        return a_ref.at[lax.rem(z + k, NZ), lax.rem(yy + NY, NY), c]

    half = NY // 2
    order = (0, NZ - 1, 1, 2)
    from_left, from_right, to_sib = {}, {}, []
    for s in range(half + 1):
        for i, k in enumerate(order):
            if s == 0:
                if k > 0:
                    z_copies[NZ - k - 1].wait_recv()
            else:
                if (s - 1, k) in from_left:
                    from_left[s - 1, k].wait_recv()
                if (s - 1, k) in from_right:
                    from_right[s - 1, k].wait_recv()
            if s < half:
                last = s == half - 1
                if not last or i % 2 == 0:
                    from_left[s, k] = send(block(k, y - s), rs.at[s, k], rr.at[s, k], right)
                if not last or i % 2 == 1:
                    from_right[s, k] = send(block(k, y + s), ls.at[s, k], lr.at[s, k], left)
            if s == 0 and k == 0:
                for copy in b_copies:
                    copy.wait_recv()
                bz = [
                    send(b_ref.at[z, :, c], bzs.at[j], bzr.at[j], z_peers[j])
                    for j in range(NZ - 1)
                ]
        to_sib.append(send(a_ref.at[:, lax.rem(y - s + NY, NY), c], ss.at[2 * s], sr.at[2 * s], sibling))
        if 0 < s < half:
            to_sib.append(
                send(a_ref.at[:, lax.rem(y + s, NY), c], ss.at[2 * s - 1], sr.at[2 * s - 1], sibling)
            )
        if s == 0:
            sib_b = [send(b_ref.at[z, :, c], bss.at[0], bsr.at[0], sibling)]
            lane = lax.broadcasted_iota(jnp.int32, tile_ref.shape, 1)
            tile = jnp.zeros(tile_ref.shape, jnp.int32)
            for t in range(owner_ref.shape[1]):
                tile = jnp.where(lane == owner_ref[0:1, t:t + 1], t, tile)
            tile_ref[...] = tile
            own[2].wait()
            one_ref[...] = onet_ref[...].T
        if s == 1:
            across.wait_recv()
            other = call_ref.at[lax.rem(n + NX, NN)]
            x_copies += [
                send(other, ns.at[k + NX], nr.at[k + NX], x_peers[k]) for k in range(NX - 1)
            ]
            for copy in t_copies:
                copy.wait_recv()
            tz = [
                send(t_ref.at[z, :, c], tzs.at[k], tzr.at[k], z_peers[k]) for k in range(NZ - 1)
            ]
            sib_t = [send(t_ref.at[z, :, c], tss.at[0], tsr.at[0], sibling)]
            own[3].wait()
            two_ref[...] = twot_ref[...].T
        if s == 2:
            own[4].wait()
            w_ref[...] = wt_ref[...].T
    for k in (NZ - 1, 1, 2):
        at = lax.rem(z + k, NZ)
        bz[NZ - k - 1].wait_recv()
        sib_b.append(send(b_ref.at[at, :, c], bss.at[k], bsr.at[k], sibling))
        tz[NZ - k - 1].wait_recv()
        sib_t.append(send(t_ref.at[at, :, c], tss.at[k], tsr.at[k], sibling))

    for copy in z_copies + b_copies + t_copies + bz + tz + [across]:
        copy.wait_send()
    for copy in list(from_left.values()) + list(from_right.values()):
        copy.wait_send()
    for copy in to_sib + sib_b + sib_t + x_copies:
        copy.wait()


def gather(owners, slots, features, cotangent, wt, onet, twot):
    rows, tokens = features.shape
    cw, ct = cotangent.shape
    width, depth = wt.shape
    half = NY // 2
    pad = rows + rows // 3
    f32, bf16 = jnp.float32, jnp.bfloat16
    a, b, t, tile, call, w, one, two = pl.pallas_call(
        gather_kernel,
        out_shape=(
            jax.ShapeDtypeStruct((NZ, NY, NC, pad, HEAD), bf16),
            jax.ShapeDtypeStruct((NZ, NY, NC, pad, KEEP - HEAD), bf16),
            jax.ShapeDtypeStruct((NZ, NY, NC, 8, 128), jnp.int32),
            jax.ShapeDtypeStruct((1, 128), jnp.int32),
            jax.ShapeDtypeStruct((NN, cw, ct), bf16),
            jax.ShapeDtypeStruct((depth, width), bf16),
            jax.ShapeDtypeStruct((depth, width), f32),
            jax.ShapeDtypeStruct((depth, width), f32),
        ),
        in_specs=[HBM] * 7,
        out_specs=(VMEM,) * 8,
        scratch_shapes=[
            pltpu.VMEM(owners.shape, jnp.int32),
            pltpu.VMEM(slots.shape, jnp.int32),
            pltpu.VMEM((rows, tokens), bf16),
            pltpu.VMEM((width, depth), bf16),
            pltpu.VMEM((width, depth), f32),
            pltpu.VMEM((width, depth), f32),
            DMA((NZ - 1,)), DMA((NZ - 1,)),
            DMA((half, NZ)), DMA((half, NZ)),
            DMA((half, NZ)), DMA((half, NZ)),
            DMA((NY + 1,)), DMA((NY + 1,)),
            DMA((NY - 1,)), DMA((NY - 1,)),
            DMA((NZ - 1,)), DMA((NZ - 1,)),
            DMA((NZ,)), DMA((NZ,)),
            DMA((NY - 1,)), DMA((NY - 1,)),
            DMA((NZ - 1,)), DMA((NZ - 1,)),
            DMA((NZ,)), DMA((NZ,)),
            DMA((NN - 1,)), DMA((NN - 1,)),
            DMA((7,)),
        ],
        compiler_params=pltpu.CompilerParams(
            collective_id=0, has_side_effects=True, vmem_limit_bytes=32 * 1024 * 1024
        ),
        name="gather_blocks",
    )(*(
        pltpu.with_memory_space_constraint(v, pltpu.HBM)
        for v in (owners, slots, features, cotangent, wt, onet, twot)
    ))
    many = NZ * NY * NC
    a, b, t = (v.reshape((many,) + v.shape[3:]) for v in (a, b, t))
    return a, b, t, tile, call, w, one, two


def arrange(a_ref, b_ref, f_ref):
    blocks, pad, _ = a_ref.shape
    rows = pad * 3 // 4
    extra = f_ref.shape[1] - KEEP

    def four(i, carry):
        at = pl.ds(pl.multiple_of(i * 4 * rows, 16), 4 * rows)
        a = a_ref[pl.ds(4 * i, 4)]
        b = b_ref[pl.ds(4 * i, 4)]
        f_ref[at, :HEAD] = jnp.concatenate([a[j, :rows] for j in range(4)], axis=0)
        f_ref[at, HEAD:KEEP] = jnp.concatenate([b[j, :rows] for j in range(4)], axis=0)
        ends = []
        for j in range(4):
            for k in range(2):
                ends.append(a[j, rows:, k * extra:(k + 1) * extra])
            ends.append(jnp.concatenate([a[j, rows:, 2 * extra:], b[j, rows:]], axis=1))
        f_ref[at, KEEP:] = jnp.concatenate(ends, axis=0)
        return carry

    lax.fori_loop(0, blocks // 4, four, 0)


def fixed_point(x):
    most = jnp.maximum(jnp.max(jnp.abs(x), axis=1, keepdims=True), LEAST)
    power = jnp.ceil(jnp.log2(most))
    q = jnp.round(x * (TOP * jnp.exp2(-power)))
    return jnp.clip(q, -TOP, TOP).astype(jnp.int32), power.astype(jnp.int32)


def code_of(x):
    a = jnp.abs(x)
    some = a >= 2.0**-126
    safe = jnp.where(some, a, 1.0)
    e = jnp.floor(jnp.log2(safe))
    code = jnp.round((e + 127.0) * 128.0 + (safe * jnp.exp2(-e) - 1.0) * 128.0)
    code = jnp.where(some, code, 0.0)
    return jnp.where(x < 0.0, -code, code).astype(jnp.int32)


def value_of(code):
    a = jnp.abs(code)
    e = lax.shift_right_logical(a, 7)
    m = lax.bitwise_and(a, 127)
    v = (1.0 + m.astype(jnp.float32) * (1.0 / 128.0)) * jnp.exp2(e.astype(jnp.float32) - 127.0)
    v = jnp.where(a == 0, 0.0, v)
    return jnp.where(code < 0, -v, v)


def exchange_kernel(
    tile_ref, a_ref, b_ref, t_ref, c_ref, wt_ref, w_ref, one_ref, two_ref,
    inbox_ref, out_ref, from_ref, f_ref, grad, outbox, share, got, total, across_got,
    send_sem, recv_sem, xs, xr, acs, acr, loc,
):
    n = lax.axis_index("node")
    w = lax.axis_index("wide")
    many = outbox.shape[0]
    partner, x_peers = node_peers_of(n, w)
    width = w_ref.shape[2]
    full = width // 128 * 128
    rest = width - full

    z, y, c = place_of(w)
    x, high = lax.rem(n, NX), n // NX

    def peer_of(i):
        step = lax.rem(i * 27, many)
        sign = 1 - 2 * c
        dz, dy, dc = place_of(step)
        to_z = lax.rem(z + NZ + sign * dz, NZ)
        to_y = lax.rem(y + NY + sign * dy, NY)
        return (to_z * NY + to_y) * NC + lax.rem(c + dc, NC), step

    barrier = pltpu.get_barrier_semaphore()
    for peer in [partner] + x_peers:
        pl.semaphore_signal(barrier, inc=1, device_id=peer, device_id_type=MESH)

    def greet(i, carry):
        p, _ = peer_of(i)
        pl.semaphore_signal(barrier, inc=1, device_id=(n, p), device_id_type=MESH)
        return carry

    lax.fori_loop(1, many, greet, 0)

    arrange(a_ref, b_ref, f_ref)
    part = grad.shape[0] // 3
    tokens = c_ref.shape[2]

    def multiply(i, carry):
        at = pl.ds(pl.multiple_of(i * part * TILE, 256), part * TILE)
        g = jnp.zeros((part * TILE, width), jnp.float32)
        for k in range(c_ref.shape[0]):
            g += lax.dot_general(
                f_ref[at, k * tokens:(k + 1) * tokens], c_ref[k],
                (((1,), (1,)), ((), ())), preferred_element_type=jnp.float32,
            )
        g = g.astype(jnp.bfloat16).astype(jnp.float32)
        grad[pl.ds(i * part, part)] = g.reshape(part, TILE, width)
        return carry

    lax.fori_loop(0, 3, multiply, 0)
    pl.semaphore_wait(barrier, many - 1 + NX)

    def pack(p):
        b = tile_ref[0, p]
        g = grad[b]
        first = 0.9 * one_ref[b] + 0.1 * g
        second = 0.999 * two_ref[b] + 0.001 * g * g
        step = first * (rate / bias_one) / (jnp.sqrt(second * (1.0 / bias_two)) + 1e-08)
        weight = (w_ref[b].astype(jnp.float32) - step).astype(jnp.bfloat16)
        qf, pf = fixed_point(first)
        qs, ps = fixed_point(second)
        cw = code_of(weight.astype(jnp.float32))
        outbox[p, :, 0:full] = qf[:, :full].astype(jnp.int16)
        outbox[p, :, full:2 * full] = qs[:, :full].astype(jnp.int16)
        outbox[p, :, 2 * full:3 * full] = cw[:, :full].astype(jnp.int16)
        lane = lax.broadcasted_iota(jnp.int32, (TILE, 128 - 3 * rest), 1)
        powers = jnp.where(lane == 0, pf, ps)
        end = jnp.concatenate([qf[:, full:], qs[:, full:], cw[:, full:], powers], axis=1)
        outbox[p, :, 3 * full:] = end.astype(jnp.int16)

    def copy_to(p, step):
        return pltpu.make_async_remote_copy(
            src_ref=outbox.at[p], dst_ref=inbox_ref.at[w],
            send_sem=send_sem.at[step], recv_sem=recv_sem.at[step],
            device_id=(n, p), device_id_type=MESH,
        )

    def send(i, carry):
        p, step = peer_of(i)
        pack(p)
        copy_to(p, step).start()
        return carry

    lax.fori_loop(1, AHEAD, send, 0)

    def partial(k, half):
        node = lax.rem(high + half, 2) * NX + lax.rem(x + k, NX)
        at = pl.ds(pl.multiple_of(node * tokens, tokens), tokens)
        share[k, half] = jnp.dot(wt_ref[...], f_ref[:, at], preferred_element_type=jnp.float32)

    x_copies = []
    for k in range(1, NX):
        for half in range(2):
            partial(k, half)
        copy = pltpu.make_async_remote_copy(
            src_ref=share.at[k], dst_ref=got.at[k - 1],
            send_sem=xs.at[k - 1], recv_sem=xr.at[k - 1],
            device_id=x_peers[k - 1], device_id_type=MESH,
        )
        copy.start()
        x_copies.append(copy)
    lax.fori_loop(AHEAD, many, send, 0)
    for half in range(2):
        partial(0, half)
    pack(w)
    mine = pltpu.make_async_copy(outbox.at[w], inbox_ref.at[w], loc)
    mine.start()

    blocks = grad.shape[0]
    lane = lax.broadcasted_iota(jnp.int32, (many, 128), 1)
    ours = jnp.logical_and(t_ref[:, 0, :] == w, lane < blocks)
    slot = jnp.min(jnp.where(ours, t_ref[:, 1, :], 128), axis=1, keepdims=True)
    source = lax.broadcasted_iota(jnp.int32, (many, 128), 0)
    from_ref[...] = jnp.max(jnp.where(slot == lane, source, -1), axis=0, keepdims=True)

    for copy in x_copies:
        copy.wait_recv()
    total[...] = share[0, 1] + got[0, 1] + got[1, 1] + got[2, 1]
    across = pltpu.make_async_remote_copy(
        src_ref=total, dst_ref=across_got, send_sem=acs, recv_sem=acr,
        device_id=partner, device_id_type=MESH,
    )
    across.start()
    near = share[0, 0] + got[0, 0] + got[1, 0] + got[2, 0]
    across.wait_recv()
    out_ref[...] = (near + across_got[...]).astype(jnp.bfloat16)

    def finish(i, carry):
        p, step = peer_of(i)
        copy_to(p, step).wait()
        return carry

    lax.fori_loop(1, many, finish, 0)
    mine.wait()
    across.wait_send()
    for copy in x_copies:
        copy.wait_send()


def exchange(tile_of, a, b, tables, cots, wt, weight, one, two):
    depth, width = weight.shape
    lanes = 3 * (width // 128 * 128) + 128
    blocks = depth // TILE
    peers = tables.shape[0]
    tokens = cots.shape[2]
    f32 = jnp.float32
    weight, one, two = (v.reshape(blocks, TILE, width) for v in (weight, one, two))
    return pl.pallas_call(
        exchange_kernel,
        out_shape=(
            jax.ShapeDtypeStruct((peers, TILE, lanes), jnp.int16),
            jax.ShapeDtypeStruct((width, tokens), jnp.bfloat16),
            jax.ShapeDtypeStruct((1, 128), jnp.int32),
        ),
        in_specs=[SMEM] + [VMEM] * 8,
        out_specs=(VMEM, VMEM, VMEM),
        scratch_shapes=[
            pltpu.VMEM((depth, tokens * NN), jnp.bfloat16),
            pltpu.VMEM((blocks, TILE, width), f32),
            pltpu.VMEM((peers, TILE, lanes), jnp.int16),
            pltpu.VMEM((NX, 2, width, tokens), f32),
            pltpu.VMEM((NX - 1, 2, width, tokens), f32),
            pltpu.VMEM((width, tokens), f32),
            pltpu.VMEM((width, tokens), f32),
            DMA((peers,)), DMA((peers,)),
            DMA((NX - 1,)), DMA((NX - 1,)),
            DMA, DMA, DMA,
        ],
        compiler_params=pltpu.CompilerParams(
            collective_id=1, has_side_effects=True, vmem_limit_bytes=32 * 1024 * 1024
        ),
        name="update_and_exchange",
    )(tile_of, a, b, tables, cots, wt, weight, one, two)


PER = 4


def place_kernel(
    from_ref, inbox_ref, total_ref, weight_out, first_out, second_out, out_ref,
    weight_ref, first_ref, second_ref, sems, last,
):
    capacity, _, width = weight_ref.shape
    full = width // 128 * 128
    rest = width - full
    whole = pltpu.make_async_copy(total_ref, out_ref, last)
    whole.start()

    def writes(i):
        at = pl.ds(i * PER, PER)
        return [
            pltpu.make_async_copy(ref.at[at], out.at[0, at], sems.at[k, i])
            for k, (ref, out) in enumerate((
                (first_ref, first_out), (second_ref, second_out), (weight_ref, weight_out),
            ))
        ]

    def some(i, carry):
        for j in range(PER):
            s = i * PER + j
            p = from_ref[0, s]
            q = jnp.where(p >= 0, inbox_ref[jnp.maximum(p, 0)].astype(jnp.int32), 0)
            end = q[:, 3 * full:]
            pf = jnp.exp2(end[:, 3 * rest:3 * rest + 1].astype(jnp.float32)) * (1.0 / TOP)
            ps = jnp.exp2(end[:, 3 * rest + 1:3 * rest + 2].astype(jnp.float32)) * (1.0 / TOP)
            first_ref[s, :, :full] = q[:, :full].astype(jnp.float32) * pf
            first_ref[s, :, full:] = end[:, :rest].astype(jnp.float32) * pf
            second_ref[s, :, :full] = q[:, full:2 * full].astype(jnp.float32) * ps
            second_ref[s, :, full:] = end[:, rest:2 * rest].astype(jnp.float32) * ps
            weight_ref[s, :, :full] = value_of(q[:, 2 * full:3 * full]).astype(jnp.bfloat16)
            weight_ref[s, :, full:] = value_of(end[:, 2 * rest:3 * rest]).astype(jnp.bfloat16)
        for copy in writes(i):
            copy.start()
        return carry

    lax.fori_loop(0, capacity // PER, some, 0)

    def finish(i, carry):
        for copy in writes(i):
            copy.wait()
        return carry

    lax.fori_loop(0, capacity // PER, finish, 0)
    whole.wait()


def place(source, inbox, total, capacity):
    shape = (1, capacity, TILE, total.shape[0])
    bf16, f32 = jnp.bfloat16, jnp.float32
    return pl.pallas_call(
        place_kernel,
        out_shape=(
            pltpu.HBM(shape, bf16),
            pltpu.HBM(shape, f32),
            pltpu.HBM(shape, f32),
            pltpu.HBM(total.shape, total.dtype),
        ),
        in_specs=[SMEM, VMEM, VMEM],
        out_specs=(HBM,) * 4,
        scratch_shapes=[
            pltpu.VMEM(shape[1:], bf16),
            pltpu.VMEM(shape[1:], f32),
            pltpu.VMEM(shape[1:], f32),
            DMA((3, capacity // PER)),
            DMA,
        ],
        compiler_params=pltpu.CompilerParams(vmem_limit_bytes=32 * 1024 * 1024),
        name="place_tiles",
    )(source, inbox, total)


def on_device(features, weight, moment_one, moment_two, cotangent, new_owner, new_slot):
    blocks = new_owner.shape[2]
    capacity = blocks + blocks // 6
    wt = weight.T
    a, b, tables, tile_of, cots, weight_rows, one, two = gather(
        new_owner[0], new_slot[0], features, cotangent.T, wt, moment_one.T, moment_two.T
    )
    inbox, total, source = exchange(tile_of, a, b, tables, cots, wt, weight_rows, one, two)
    *moved, projected = place(source, inbox, total, capacity)
    return (projected.T,) + tuple(moved)


def solution(mesh):
    placed = (
        P(("node", "wide"), None),
        P("node", "wide"),
        P("node", "wide"),
        P("node", "wide"),
        P("node", "wide"),
        P("node", "wide", None),
        P("node", "wide", None),
    )
    return jax.shard_map(
        on_device,
        mesh=mesh,
        in_specs=placed,
        out_specs=(
            P("node", "wide"),
            P("node", "wide", None, None),
            P("node", "wide", None, None),
            P("node", "wide", None, None),
        ),
        check_vma=False,
    )
```

```python
import jax
import jax.numpy as jnp
from jax import lax
from jax.experimental import pallas as pl
from jax.experimental.pallas import tpu as pltpu
from jax.sharding import PartitionSpec as P

TILE = 32
NZ, NY, NC = 4, 8, 2
NX = 4
NN = 2 * NX
MESH = pl.DeviceIdType.MESH
ANY = pl.BlockSpec(memory_space=pl.ANY)
HBM = pl.BlockSpec(memory_space=pltpu.HBM)
VMEM = pl.BlockSpec(memory_space=pltpu.VMEM)
SMEM = pl.BlockSpec(memory_space=pltpu.SMEM)
DMA = pltpu.SemaphoreType.DMA

rate = 0.02
bias_one = 1.0 - 0.9**10
bias_two = 1.0 - 0.999**10

TOP = 32767.0
LEAST = 2.0**-100


def place_of(w):
    return w // (NY * NC), (w // NC) % NY, w % NC


def node_peers_of(n, w):
    x = lax.rem(n, NX)
    base = n - x
    return (lax.rem(n + NX, NN), w), [(base + lax.rem(x + k, NX), w) for k in range(1, NX)]


HEAD = 1280
AHEAD = 9
KEEP = 1536


def gather_part(
    owner_smem, owner_in, slot_in, x_in, c_in, wt_in, onet_in, twot_in,
    a_ref, b_ref, t_ref, tile_ref, call_ref, w_ref, one_ref, two_ref,
    owner_ref, slot_ref, x_ref, wt_ref, onet_ref, twot_ref,
    zs, zr, rs, rr, ls, lr, ss, sr, bs, br, bzs, bzr, bss, bsr,
    ts, tr, tzs, tzr, tss, tsr, ns, nr, loc,
):
    n = lax.axis_index("node")
    w = lax.axis_index("wide")
    z, y, c = place_of(w)

    def wide(zz, yy, cc):
        return (n, (lax.rem(zz + NZ, NZ) * NY + lax.rem(yy + NY, NY)) * NC + cc)

    sibling = wide(z, y, 1 - c)
    y_peers = [wide(z, y + k, c) for k in range(1, NY)]
    right, left = y_peers[0], y_peers[-1]
    z_peers = [wide(z + k, y, c) for k in range(1, NZ)]
    partner, x_peers = node_peers_of(n, w)

    barrier = pltpu.get_barrier_semaphore()
    for peer in [partner] + x_peers:
        pl.semaphore_signal(barrier, inc=1, device_id=peer, device_id_type=MESH)
    many = NZ * NY * NC

    def greet(i, carry):
        pl.semaphore_signal(
            barrier, inc=1, device_id=(n, lax.rem(w + i, many)), device_id_type=MESH
        )
        return carry

    lax.fori_loop(1, many, greet, 0)

    own = [
        pltpu.make_async_copy(src, dst, loc.at[i])
        for i, (src, dst) in enumerate((
            (x_in, x_ref), (c_in, call_ref.at[n]),
            (onet_in, onet_ref), (twot_in, twot_ref), (wt_in, wt_ref),
            (owner_in, owner_ref), (slot_in, slot_ref),
        ))
    ]
    for copy in own:
        copy.start()
    own[0].wait()

    rows = x_ref.shape[0]
    extra = x_ref.shape[1] - KEEP
    third = HEAD - 2 * extra
    a_ref[z, y, c, :rows, :] = x_ref[:, :HEAD]
    b_ref[z, y, c, :rows, :] = x_ref[:, HEAD:KEEP]
    for k in range(2):
        a_ref[z, y, c, rows:, k * extra:(k + 1) * extra] = x_ref[4 * k:4 * k + 4, KEEP:]
    a_ref[z, y, c, rows:, 2 * extra:] = x_ref[rows - 4:, KEEP:KEEP + third]
    b_ref[z, y, c, rows:, :] = x_ref[rows - 4:, KEEP + third:]
    own[5].wait()
    own[6].wait()
    t_ref[z, y, c, 0:1, :owner_ref.shape[1]] = owner_ref[...]
    t_ref[z, y, c, 1:2, :slot_ref.shape[1]] = slot_ref[...]
    own[1].wait()

    pl.semaphore_wait(barrier, many - 1 + NX)

    def send(ref, s, r, peer):
        copy = pltpu.make_async_remote_copy(
            src_ref=ref, dst_ref=ref, send_sem=s, recv_sem=r,
            device_id=peer, device_id_type=MESH,
        )
        copy.start()
        return copy

    b_copies = [
        send(b_ref.at[z, y, c], bs.at[k], br.at[k], y_peers[k]) for k in range(NY - 1)
    ]
    z_copies = [
        send(a_ref.at[z, y, c], zs.at[k], zr.at[k], z_peers[k]) for k in range(NZ - 1)
    ]
    across = send(call_ref.at[n], ns.at[0], nr.at[0], partner)
    x_copies = [
        send(call_ref.at[n], ns.at[k + 1], nr.at[k + 1], x_peers[k]) for k in range(NX - 1)
    ]
    t_copies = [
        send(t_ref.at[z, y, c], ts.at[k], tr.at[k], y_peers[k]) for k in range(NY - 1)
    ]

    def block(k, yy):
        return a_ref.at[lax.rem(z + k, NZ), lax.rem(yy + NY, NY), c]

    half = NY // 2
    order = (0, NZ - 1, 1, 2)
    from_left, from_right, to_sib = {}, {}, []
    for s in range(half + 1):
        for i, k in enumerate(order):
            if s == 0:
                if k > 0:
                    z_copies[NZ - k - 1].wait_recv()
            else:
                if (s - 1, k) in from_left:
                    from_left[s - 1, k].wait_recv()
                if (s - 1, k) in from_right:
                    from_right[s - 1, k].wait_recv()
            if s < half:
                last = s == half - 1
                if not last or i % 2 == 0:
                    from_left[s, k] = send(block(k, y - s), rs.at[s, k], rr.at[s, k], right)
                if not last or i % 2 == 1:
                    from_right[s, k] = send(block(k, y + s), ls.at[s, k], lr.at[s, k], left)
            if s == 0 and k == 0:
                for copy in b_copies:
                    copy.wait_recv()
                bz = [
                    send(b_ref.at[z, :, c], bzs.at[j], bzr.at[j], z_peers[j])
                    for j in range(NZ - 1)
                ]
        to_sib.append(send(a_ref.at[:, lax.rem(y - s + NY, NY), c], ss.at[2 * s], sr.at[2 * s], sibling))
        if 0 < s < half:
            to_sib.append(
                send(a_ref.at[:, lax.rem(y + s, NY), c], ss.at[2 * s - 1], sr.at[2 * s - 1], sibling)
            )
        if s == 0:
            sib_b = [send(b_ref.at[z, :, c], bss.at[0], bsr.at[0], sibling)]
            def tile_at(p, carry):
                tile = 0
                for t in range(owner_ref.shape[1]):
                    tile = jnp.where(owner_smem[0, t] == p, t, tile)
                tile_ref[p] = tile
                return carry

            lax.fori_loop(0, many, tile_at, 0)
            own[2].wait()
            one_ref[...] = onet_ref[...].T.reshape(one_ref.shape)
        if s == 1:
            across.wait_recv()
            other = call_ref.at[lax.rem(n + NX, NN)]
            x_copies += [
                send(other, ns.at[k + NX], nr.at[k + NX], x_peers[k]) for k in range(NX - 1)
            ]
            for copy in t_copies:
                copy.wait_recv()
            tz = [
                send(t_ref.at[z, :, c], tzs.at[k], tzr.at[k], z_peers[k]) for k in range(NZ - 1)
            ]
            sib_t = [send(t_ref.at[z, :, c], tss.at[0], tsr.at[0], sibling)]
            own[3].wait()
            two_ref[...] = twot_ref[...].T.reshape(two_ref.shape)
        if s == 2:
            own[4].wait()
            w_ref[...] = wt_ref[...].T.reshape(w_ref.shape)
    for k in (NZ - 1, 1, 2):
        at = lax.rem(z + k, NZ)
        bz[NZ - k - 1].wait_recv()
        sib_b.append(send(b_ref.at[at, :, c], bss.at[k], bsr.at[k], sibling))
        tz[NZ - k - 1].wait_recv()
        sib_t.append(send(t_ref.at[at, :, c], tss.at[k], tsr.at[k], sibling))

    for copy in z_copies + b_copies + t_copies + bz + tz + [across]:
        copy.wait_send()
    for copy in list(from_left.values()) + list(from_right.values()):
        copy.wait_send()
    for copy in to_sib + sib_b + sib_t + x_copies:
        copy.wait()


def arrange(a_ref, b_ref, f_ref):
    pad = a_ref.shape[3]
    rows = pad * 3 // 4
    extra = f_ref.shape[1] - KEEP

    def four(i, carry):
        at = pl.ds(pl.multiple_of(i * 4 * rows, 16), 4 * rows)
        ys = pl.ds(lax.rem(i, NY // 2) * 2, 2)
        a = a_ref[i // (NY // 2), ys]
        b = b_ref[i // (NY // 2), ys]
        a = a.reshape((4,) + a.shape[2:])
        b = b.reshape((4,) + b.shape[2:])
        f_ref[at, :HEAD] = jnp.concatenate([a[j, :rows] for j in range(4)], axis=0)
        f_ref[at, HEAD:KEEP] = jnp.concatenate([b[j, :rows] for j in range(4)], axis=0)
        ends = []
        for j in range(4):
            for k in range(2):
                ends.append(a[j, rows:, k * extra:(k + 1) * extra])
            ends.append(jnp.concatenate([a[j, rows:, 2 * extra:], b[j, rows:]], axis=1))
        f_ref[at, KEEP:] = jnp.concatenate(ends, axis=0)
        return carry

    lax.fori_loop(0, NZ * NY * NC // 4, four, 0)


def fixed_point(x):
    most = jnp.maximum(jnp.max(jnp.abs(x), axis=1, keepdims=True), LEAST)
    power = jnp.ceil(jnp.log2(most))
    q = jnp.round(x * (TOP * jnp.exp2(-power)))
    return jnp.clip(q, -TOP, TOP).astype(jnp.int32), power.astype(jnp.int32)


def code_of(x):
    a = jnp.abs(x)
    some = a >= 2.0**-126
    safe = jnp.where(some, a, 1.0)
    e = jnp.floor(jnp.log2(safe))
    code = jnp.round((e + 127.0) * 128.0 + (safe * jnp.exp2(-e) - 1.0) * 128.0)
    code = jnp.where(some, code, 0.0)
    return jnp.where(x < 0.0, -code, code).astype(jnp.int32)


def value_of(code):
    a = jnp.abs(code)
    e = lax.shift_right_logical(a, 7)
    m = lax.bitwise_and(a, 127)
    v = (1.0 + m.astype(jnp.float32) * (1.0 / 128.0)) * jnp.exp2(e.astype(jnp.float32) - 127.0)
    v = jnp.where(a == 0, 0.0, v)
    return jnp.where(code < 0, -v, v)


def exchange_part(
    tile_ref, a_ref, b_ref, t_ref, c_ref, wt_ref, w_ref, one_ref, two_ref,
    inbox_ref, out_ref, from_ref, f_ref, grad, outbox, share, got, total, across_got,
    send_sem, recv_sem, xs, xr, acs, acr, loc,
):
    n = lax.axis_index("node")
    w = lax.axis_index("wide")
    many = outbox.shape[0]
    partner, x_peers = node_peers_of(n, w)
    width = w_ref.shape[2]
    full = width // 128 * 128
    rest = width - full

    z, y, c = place_of(w)
    x, high = lax.rem(n, NX), n // NX

    def peer_of(i):
        step = lax.rem(i * 27, many)
        sign = 1 - 2 * c
        dz, dy, dc = place_of(step)
        to_z = lax.rem(z + NZ + sign * dz, NZ)
        to_y = lax.rem(y + NY + sign * dy, NY)
        return (to_z * NY + to_y) * NC + lax.rem(c + dc, NC), step

    arrange(a_ref, b_ref, f_ref)
    part = grad.shape[0] // 3
    tokens = c_ref.shape[2]

    def multiply(i, carry):
        at = pl.ds(pl.multiple_of(i * part * TILE, 256), part * TILE)
        g = jnp.zeros((part * TILE, width), jnp.float32)
        for k in range(c_ref.shape[0]):
            g += lax.dot_general(
                f_ref[at, k * tokens:(k + 1) * tokens], c_ref[k],
                (((1,), (1,)), ((), ())), preferred_element_type=jnp.float32,
            )
        g = g.astype(jnp.bfloat16).astype(jnp.float32)
        grad[pl.ds(i * part, part)] = g.reshape(part, TILE, width)
        return carry

    lax.fori_loop(0, 3, multiply, 0)

    def pack(p):
        b = tile_ref[p]
        g = grad[b]
        first = 0.9 * one_ref[b] + 0.1 * g
        second = 0.999 * two_ref[b] + 0.001 * g * g
        step = first * (rate / bias_one) / (jnp.sqrt(second * (1.0 / bias_two)) + 1e-08)
        weight = (w_ref[b].astype(jnp.float32) - step).astype(jnp.bfloat16)
        qf, pf = fixed_point(first)
        qs, ps = fixed_point(second)
        cw = code_of(weight.astype(jnp.float32))
        outbox[p, :, 0:full] = qf[:, :full].astype(jnp.int16)
        outbox[p, :, full:2 * full] = qs[:, :full].astype(jnp.int16)
        outbox[p, :, 2 * full:3 * full] = cw[:, :full].astype(jnp.int16)
        lane = lax.broadcasted_iota(jnp.int32, (TILE, 128 - 3 * rest), 1)
        powers = jnp.where(lane == 0, pf, ps)
        end = jnp.concatenate([qf[:, full:], qs[:, full:], cw[:, full:], powers], axis=1)
        outbox[p, :, 3 * full:] = end.astype(jnp.int16)

    def copy_to(p, step):
        return pltpu.make_async_remote_copy(
            src_ref=outbox.at[p], dst_ref=inbox_ref.at[w],
            send_sem=send_sem.at[step], recv_sem=recv_sem.at[step],
            device_id=(n, p), device_id_type=MESH,
        )

    def send(i, carry):
        p, step = peer_of(i)
        pack(p)
        copy_to(p, step).start()
        return carry

    lax.fori_loop(1, AHEAD, send, 0)

    def partial(k, half):
        node = lax.rem(high + half, 2) * NX + lax.rem(x + k, NX)
        at = pl.ds(pl.multiple_of(node * tokens, tokens), tokens)
        share[k, half] = jnp.dot(wt_ref[...], f_ref[:, at], preferred_element_type=jnp.float32)

    x_copies = []
    for k in range(1, NX):
        for half in range(2):
            partial(k, half)
        copy = pltpu.make_async_remote_copy(
            src_ref=share.at[k], dst_ref=got.at[k - 1],
            send_sem=xs.at[k - 1], recv_sem=xr.at[k - 1],
            device_id=x_peers[k - 1], device_id_type=MESH,
        )
        copy.start()
        x_copies.append(copy)
    lax.fori_loop(AHEAD, many, send, 0)
    for half in range(2):
        partial(0, half)
    pack(w)
    mine = pltpu.make_async_copy(outbox.at[w], inbox_ref.at[w], loc)
    mine.start()

    blocks = grad.shape[0]
    lane = lax.broadcasted_iota(jnp.int32, (many, 128), 1)
    tables = t_ref[...].reshape((many,) + t_ref.shape[3:])
    ours = jnp.logical_and(tables[:, 0, :] == w, lane < blocks)
    slot = jnp.min(jnp.where(ours, tables[:, 1, :], 128), axis=1, keepdims=True)
    source = lax.broadcasted_iota(jnp.int32, (many, 128), 0)
    from_ref[...] = jnp.max(jnp.where(slot == lane, source, -1), axis=0, keepdims=True)

    for copy in x_copies:
        copy.wait_recv()
    total[...] = share[0, 1] + got[0, 1] + got[1, 1] + got[2, 1]
    across = pltpu.make_async_remote_copy(
        src_ref=total, dst_ref=across_got, send_sem=acs, recv_sem=acr,
        device_id=partner, device_id_type=MESH,
    )
    across.start()
    near = share[0, 0] + got[0, 0] + got[1, 0] + got[2, 0]
    across.wait_recv()
    out_ref[...] = (near + across_got[...]).astype(jnp.bfloat16)

    def finish(i, carry):
        p, step = peer_of(i)
        copy_to(p, step).wait()
        return carry

    lax.fori_loop(1, many, finish, 0)
    mine.wait()
    across.wait_send()
    for copy in x_copies:
        copy.wait_send()


def step_kernel(*refs):
    ins, outs, held, rest = refs[:8], refs[8:11], refs[11:25], refs[25:]
    (a_ref, b_ref, t_ref, tile_ref, call_ref, w_ref, one_ref, two_ref,
     owner_ref, slot_ref, x_ref, wt_ref, onet_ref, twot_ref) = held
    gather_part(*ins, *held, *rest[:23])
    exchange_part(
        tile_ref, a_ref, b_ref, t_ref, call_ref, wt_ref, w_ref, one_ref, two_ref,
        *outs, *rest[23:],
    )


def step(owners, slots, features, cotangent, wt, onet, twot):
    rows = features.shape[0]
    width, tokens = cotangent.shape
    depth = wt.shape[1]
    half = NY // 2
    pad = rows + rows // 3
    peers = NZ * NY * NC
    blocks = depth // TILE
    lanes = 3 * (width // 128 * 128) + 128
    i16, i32, f32, bf16 = jnp.int16, jnp.int32, jnp.float32, jnp.bfloat16
    return pl.pallas_call(
        step_kernel,
        out_shape=(
            jax.ShapeDtypeStruct((peers, TILE, lanes), i16),
            jax.ShapeDtypeStruct((width, tokens), bf16),
            jax.ShapeDtypeStruct((1, 128), i32),
        ),
        in_specs=[SMEM] + [HBM] * 7,
        out_specs=(VMEM,) * 3,
        scratch_shapes=[
            pltpu.VMEM((NZ, NY, NC, pad, HEAD), bf16),
            pltpu.VMEM((NZ, NY, NC, pad, KEEP - HEAD), bf16),
            pltpu.VMEM((NZ, NY, NC, 8, 128), i32),
            pltpu.SMEM((peers,), i32),
            pltpu.VMEM((NN, width, tokens), bf16),
            pltpu.VMEM((blocks, TILE, width), bf16),
            pltpu.VMEM((blocks, TILE, width), f32),
            pltpu.VMEM((blocks, TILE, width), f32),
            pltpu.VMEM(owners.shape, i32),
            pltpu.VMEM(slots.shape, i32),
            pltpu.VMEM(features.shape, bf16),
            pltpu.VMEM((width, depth), bf16),
            pltpu.VMEM((width, depth), f32),
            pltpu.VMEM((width, depth), f32),
            DMA((NZ - 1,)), DMA((NZ - 1,)),
            DMA((half, NZ)), DMA((half, NZ)),
            DMA((half, NZ)), DMA((half, NZ)),
            DMA((NY + 1,)), DMA((NY + 1,)),
            DMA((NY - 1,)), DMA((NY - 1,)),
            DMA((NZ - 1,)), DMA((NZ - 1,)),
            DMA((NZ,)), DMA((NZ,)),
            DMA((NY - 1,)), DMA((NY - 1,)),
            DMA((NZ - 1,)), DMA((NZ - 1,)),
            DMA((NZ,)), DMA((NZ,)),
            DMA((NN - 1,)), DMA((NN - 1,)),
            DMA((7,)),
            pltpu.VMEM((depth, tokens * NN), bf16),
            pltpu.VMEM((blocks, TILE, width), f32),
            pltpu.VMEM((peers, TILE, lanes), i16),
            pltpu.VMEM((NX, 2, width, tokens), f32),
            pltpu.VMEM((NX - 1, 2, width, tokens), f32),
            pltpu.VMEM((width, tokens), f32),
            pltpu.VMEM((width, tokens), f32),
            DMA((peers,)), DMA((peers,)),
            DMA((NX - 1,)), DMA((NX - 1,)),
            DMA, DMA, DMA,
        ],
        compiler_params=pltpu.CompilerParams(
            collective_id=0, has_side_effects=True, vmem_limit_bytes=48 * 1024 * 1024
        ),
        name="gather_update_exchange",
    )(owners, *(
        pltpu.with_memory_space_constraint(v, pltpu.HBM)
        for v in (owners, slots, features, cotangent, wt, onet, twot)
    ))


PER = 4


def place_kernel(
    from_ref, inbox_ref, total_ref, weight_out, first_out, second_out, out_ref,
    weight_ref, first_ref, second_ref, sems, last,
):
    capacity, _, width = weight_ref.shape
    full = width // 128 * 128
    rest = width - full
    whole = pltpu.make_async_copy(total_ref, out_ref, last)
    whole.start()

    def writes(i):
        at = pl.ds(i * PER, PER)
        return [
            pltpu.make_async_copy(ref.at[at], out.at[0, at], sems.at[k, i])
            for k, (ref, out) in enumerate((
                (first_ref, first_out), (second_ref, second_out), (weight_ref, weight_out),
            ))
        ]

    def some(i, carry):
        for j in range(PER):
            s = i * PER + j
            p = from_ref[0, s]
            q = jnp.where(p >= 0, inbox_ref[jnp.maximum(p, 0)].astype(jnp.int32), 0)
            end = q[:, 3 * full:]
            pf = jnp.exp2(end[:, 3 * rest:3 * rest + 1].astype(jnp.float32)) * (1.0 / TOP)
            ps = jnp.exp2(end[:, 3 * rest + 1:3 * rest + 2].astype(jnp.float32)) * (1.0 / TOP)
            first_ref[s, :, :full] = q[:, :full].astype(jnp.float32) * pf
            first_ref[s, :, full:] = end[:, :rest].astype(jnp.float32) * pf
            second_ref[s, :, :full] = q[:, full:2 * full].astype(jnp.float32) * ps
            second_ref[s, :, full:] = end[:, rest:2 * rest].astype(jnp.float32) * ps
            weight_ref[s, :, :full] = value_of(q[:, 2 * full:3 * full]).astype(jnp.bfloat16)
            weight_ref[s, :, full:] = value_of(end[:, 2 * rest:3 * rest]).astype(jnp.bfloat16)
        for copy in writes(i):
            copy.start()
        return carry

    lax.fori_loop(0, capacity // PER, some, 0)

    def finish(i, carry):
        for copy in writes(i):
            copy.wait()
        return carry

    lax.fori_loop(0, capacity // PER, finish, 0)
    whole.wait()


def place(source, inbox, total, capacity):
    shape = (1, capacity, TILE, total.shape[0])
    bf16, f32 = jnp.bfloat16, jnp.float32
    return pl.pallas_call(
        place_kernel,
        out_shape=(
            pltpu.HBM(shape, bf16),
            pltpu.HBM(shape, f32),
            pltpu.HBM(shape, f32),
            pltpu.HBM(total.shape, total.dtype),
        ),
        in_specs=[SMEM, VMEM, VMEM],
        out_specs=(HBM,) * 4,
        scratch_shapes=[
            pltpu.VMEM(shape[1:], bf16),
            pltpu.VMEM(shape[1:], f32),
            pltpu.VMEM(shape[1:], f32),
            DMA((3, capacity // PER)),
            DMA,
        ],
        compiler_params=pltpu.CompilerParams(vmem_limit_bytes=32 * 1024 * 1024),
        name="place_tiles",
    )(source, inbox, total)


def on_device(features, weight, moment_one, moment_two, cotangent, new_owner, new_slot):
    blocks = new_owner.shape[2]
    capacity = blocks + blocks // 6
    inbox, total, source = step(
        new_owner[0], new_slot[0], features, cotangent.T, weight.T, moment_one.T, moment_two.T
    )
    *moved, projected = place(source, inbox, total, capacity)
    return (projected.T,) + tuple(moved)


def solution(mesh):
    placed = (
        P(("node", "wide"), None),
        P("node", "wide"),
        P("node", "wide"),
        P("node", "wide"),
        P("node", "wide"),
        P("node", "wide", None),
        P("node", "wide", None),
    )
    return jax.shard_map(
        on_device,
        mesh=mesh,
        in_specs=placed,
        out_specs=(
            P("node", "wide"),
            P("node", "wide", None, None),
            P("node", "wide", None, None),
            P("node", "wide", None, None),
        ),
        check_vma=False,
    )
```

```python
import jax
import jax.numpy as jnp
from jax import lax
from jax.experimental import pallas as pl
from jax.experimental.pallas import tpu as pltpu
from jax.sharding import PartitionSpec as P

TILE = 32
NZ, NY, NC = 4, 8, 2
NX = 4
NN = 2 * NX
MESH = pl.DeviceIdType.MESH
ANY = pl.BlockSpec(memory_space=pl.ANY)
HBM = pl.BlockSpec(memory_space=pltpu.HBM)
VMEM = pl.BlockSpec(memory_space=pltpu.VMEM)
SMEM = pl.BlockSpec(memory_space=pltpu.SMEM)
DMA = pltpu.SemaphoreType.DMA

rate = 0.02
bias_one = 1.0 - 0.9**10
bias_two = 1.0 - 0.999**10

TOP = 32767.0
LEAST = 2.0**-100


def place_of(w):
    return w // (NY * NC), (w // NC) % NY, w % NC


def node_peers_of(n, w):
    x = lax.rem(n, NX)
    base = n - x
    return (lax.rem(n + NX, NN), w), [(base + lax.rem(x + k, NX), w) for k in range(1, NX)]


HEAD = 1280
AHEAD = 9
KEEP = 1536


def gather_part(
    owner_smem, owner_in, slot_in, x_in, c_in, wt_in, onet_in, twot_in,
    a_ref, b_ref, t_ref, tile_ref, call_ref, w_ref, one_ref, two_ref,
    owner_ref, slot_ref, x_ref, wt_ref, onet_ref, twot_ref,
    zs, zr, rs, rr, ls, lr, ss, sr, bs, br, bzs, bzr, bss, bsr,
    ts, tr, tzs, tzr, tss, tsr, ns, nr, loc,
):
    n = lax.axis_index("node")
    w = lax.axis_index("wide")
    z, y, c = place_of(w)

    def wide(zz, yy, cc):
        return (n, (lax.rem(zz + NZ, NZ) * NY + lax.rem(yy + NY, NY)) * NC + cc)

    sibling = wide(z, y, 1 - c)
    y_peers = [wide(z, y + k, c) for k in range(1, NY)]
    right, left = y_peers[0], y_peers[-1]
    z_peers = [wide(z + k, y, c) for k in range(1, NZ)]
    partner, x_peers = node_peers_of(n, w)

    barrier = pltpu.get_barrier_semaphore()
    for peer in [partner] + x_peers:
        pl.semaphore_signal(barrier, inc=1, device_id=peer, device_id_type=MESH)
    many = NZ * NY * NC

    def greet(i, carry):
        pl.semaphore_signal(
            barrier, inc=1, device_id=(n, lax.rem(w + i, many)), device_id_type=MESH
        )
        return carry

    lax.fori_loop(1, many, greet, 0)

    own = [
        pltpu.make_async_copy(src, dst, loc.at[i])
        for i, (src, dst) in enumerate((
            (x_in, x_ref), (c_in, call_ref.at[n]),
            (onet_in, onet_ref), (twot_in, twot_ref), (wt_in, wt_ref),
            (owner_in, owner_ref), (slot_in, slot_ref),
        ))
    ]
    for copy in own:
        copy.start()
    own[0].wait()

    rows = x_ref.shape[0]
    extra = x_ref.shape[1] - KEEP
    third = HEAD - 2 * extra
    a_ref[z, y, c, :rows, :] = x_ref[:, :HEAD]
    b_ref[z, y, c, :rows, :] = x_ref[:, HEAD:KEEP]
    for k in range(2):
        a_ref[z, y, c, rows:, k * extra:(k + 1) * extra] = x_ref[4 * k:4 * k + 4, KEEP:]
    a_ref[z, y, c, rows:, 2 * extra:] = x_ref[rows - 4:, KEEP:KEEP + third]
    b_ref[z, y, c, rows:, :] = x_ref[rows - 4:, KEEP + third:]
    own[5].wait()
    own[6].wait()
    t_ref[z, y, c, 0:1, :owner_ref.shape[1]] = owner_ref[...]
    t_ref[z, y, c, 1:2, :slot_ref.shape[1]] = slot_ref[...]
    own[1].wait()

    pl.semaphore_wait(barrier, many - 1 + NX)

    def send(ref, s, r, peer):
        copy = pltpu.make_async_remote_copy(
            src_ref=ref, dst_ref=ref, send_sem=s, recv_sem=r,
            device_id=peer, device_id_type=MESH,
        )
        copy.start()
        return copy

    b_copies = [
        send(b_ref.at[z, y, c], bs.at[k], br.at[k], y_peers[k]) for k in range(NY - 1)
    ]
    z_copies = [
        send(a_ref.at[z, y, c], zs.at[k], zr.at[k], z_peers[k]) for k in range(NZ - 1)
    ]
    across = send(call_ref.at[n], ns.at[0], nr.at[0], partner)
    x_copies = [
        send(call_ref.at[n], ns.at[k + 1], nr.at[k + 1], x_peers[k]) for k in range(NX - 1)
    ]
    t_copies = [
        send(t_ref.at[z, y, c], ts.at[k], tr.at[k], y_peers[k]) for k in range(NY - 1)
    ]

    def block(k, yy):
        return a_ref.at[lax.rem(z + k, NZ), lax.rem(yy + NY, NY), c]

    half = NY // 2
    order = (0, NZ - 1, 1, 2)
    from_left, from_right, to_sib = {}, {}, []
    for s in range(half + 1):
        for i, k in enumerate(order):
            if s == 0:
                if k > 0:
                    z_copies[NZ - k - 1].wait_recv()
            else:
                if (s - 1, k) in from_left:
                    from_left[s - 1, k].wait_recv()
                if (s - 1, k) in from_right:
                    from_right[s - 1, k].wait_recv()
            if s < half:
                last = s == half - 1
                if not last or i % 2 == 0:
                    from_left[s, k] = send(block(k, y - s), rs.at[s, k], rr.at[s, k], right)
                if not last or i % 2 == 1:
                    from_right[s, k] = send(block(k, y + s), ls.at[s, k], lr.at[s, k], left)
            if s == 0 and k == 0:
                for copy in b_copies:
                    copy.wait_recv()
                bz = [
                    send(b_ref.at[z, :, c], bzs.at[j], bzr.at[j], z_peers[j])
                    for j in range(NZ - 1)
                ]
        to_sib.append(send(a_ref.at[:, lax.rem(y - s + NY, NY), c], ss.at[2 * s], sr.at[2 * s], sibling))
        if 0 < s < half:
            to_sib.append(
                send(a_ref.at[:, lax.rem(y + s, NY), c], ss.at[2 * s - 1], sr.at[2 * s - 1], sibling)
            )
        if s == 0:
            sib_b = [send(b_ref.at[z, :, c], bss.at[0], bsr.at[0], sibling)]
            def tile_at(p, carry):
                tile = 0
                for t in range(owner_ref.shape[1]):
                    tile = jnp.where(owner_smem[0, t] == p, t, tile)
                tile_ref[p] = tile
                return carry

            lax.fori_loop(0, many, tile_at, 0)
            own[2].wait()
            one_ref[...] = onet_ref[...].T.reshape(one_ref.shape)
        if s == 1:
            across.wait_recv()
            other = call_ref.at[lax.rem(n + NX, NN)]
            x_copies += [
                send(other, ns.at[k + NX], nr.at[k + NX], x_peers[k]) for k in range(NX - 1)
            ]
            for copy in t_copies:
                copy.wait_recv()
            tz = [
                send(t_ref.at[z, :, c], tzs.at[k], tzr.at[k], z_peers[k]) for k in range(NZ - 1)
            ]
            sib_t = [send(t_ref.at[z, :, c], tss.at[0], tsr.at[0], sibling)]
            own[3].wait()
            two_ref[...] = twot_ref[...].T.reshape(two_ref.shape)
        if s == 2:
            own[4].wait()
            w_ref[...] = wt_ref[...].T.reshape(w_ref.shape)
    for k in (NZ - 1, 1, 2):
        at = lax.rem(z + k, NZ)
        bz[NZ - k - 1].wait_recv()
        sib_b.append(send(b_ref.at[at, :, c], bss.at[k], bsr.at[k], sibling))
        tz[NZ - k - 1].wait_recv()
        sib_t.append(send(t_ref.at[at, :, c], tss.at[k], tsr.at[k], sibling))

    for copy in z_copies + b_copies + t_copies + bz + tz + [across]:
        copy.wait_send()
    for copy in list(from_left.values()) + list(from_right.values()):
        copy.wait_send()
    for copy in to_sib + sib_b + sib_t + x_copies:
        copy.wait()


def arrange(a_ref, b_ref, f_ref):
    pad = a_ref.shape[3]
    rows = pad * 3 // 4
    extra = f_ref.shape[1] - KEEP

    def four(i, carry):
        at = pl.ds(pl.multiple_of(i * 4 * rows, 16), 4 * rows)
        ys = pl.ds(lax.rem(i, NY // 2) * 2, 2)
        a = a_ref[i // (NY // 2), ys]
        b = b_ref[i // (NY // 2), ys]
        a = a.reshape((4,) + a.shape[2:])
        b = b.reshape((4,) + b.shape[2:])
        f_ref[at, :HEAD] = jnp.concatenate([a[j, :rows] for j in range(4)], axis=0)
        f_ref[at, HEAD:KEEP] = jnp.concatenate([b[j, :rows] for j in range(4)], axis=0)
        ends = []
        for j in range(4):
            for k in range(2):
                ends.append(a[j, rows:, k * extra:(k + 1) * extra])
            ends.append(jnp.concatenate([a[j, rows:, 2 * extra:], b[j, rows:]], axis=1))
        f_ref[at, KEEP:] = jnp.concatenate(ends, axis=0)
        return carry

    lax.fori_loop(0, NZ * NY * NC // 4, four, 0)


def fixed_point(x):
    most = jnp.maximum(jnp.max(jnp.abs(x), axis=1, keepdims=True), LEAST)
    power = jnp.ceil(jnp.log2(most))
    q = jnp.round(x * (TOP * jnp.exp2(-power)))
    return jnp.clip(q, -TOP, TOP).astype(jnp.int32), power.astype(jnp.int32)


def code_of(x):
    a = jnp.abs(x)
    some = a >= 2.0**-126
    safe = jnp.where(some, a, 1.0)
    e = jnp.floor(jnp.log2(safe))
    code = jnp.round((e + 127.0) * 128.0 + (safe * jnp.exp2(-e) - 1.0) * 128.0)
    code = jnp.where(some, code, 0.0)
    return jnp.where(x < 0.0, -code, code).astype(jnp.int32)


def value_of(code):
    a = jnp.abs(code)
    e = lax.shift_right_logical(a, 7)
    m = lax.bitwise_and(a, 127)
    v = (1.0 + m.astype(jnp.float32) * (1.0 / 128.0)) * jnp.exp2(e.astype(jnp.float32) - 127.0)
    v = jnp.where(a == 0, 0.0, v)
    return jnp.where(code < 0, -v, v)


def exchange_part(
    tile_ref, a_ref, b_ref, t_ref, c_ref, wt_ref, w_ref, one_ref, two_ref,
    inbox_ref, out_ref, from_ref, f_ref, grad, outbox, share, got, total, across_got,
    send_sem, recv_sem, xs, xr, acs, acr, loc,
):
    n = lax.axis_index("node")
    w = lax.axis_index("wide")
    many = outbox.shape[0]
    partner, x_peers = node_peers_of(n, w)
    width = w_ref.shape[2]
    full = width // 128 * 128
    rest = width - full

    z, y, c = place_of(w)
    x, high = lax.rem(n, NX), n // NX

    def peer_of(i):
        step = lax.rem(i * 45, many)
        sign = 1 - 2 * c
        dz, dy, dc = place_of(step)
        to_z = lax.rem(z + NZ + sign * dz, NZ)
        to_y = lax.rem(y + NY + sign * dy, NY)
        return (to_z * NY + to_y) * NC + lax.rem(c + dc, NC), step

    arrange(a_ref, b_ref, f_ref)
    part = grad.shape[0] // 3
    tokens = c_ref.shape[2]

    def multiply(i, carry):
        at = pl.ds(pl.multiple_of(i * part * TILE, 256), part * TILE)
        g = jnp.zeros((width, part * TILE), jnp.float32)
        for k in range(c_ref.shape[0]):
            g += lax.dot_general(
                c_ref[k], f_ref[at, k * tokens:(k + 1) * tokens],
                (((1,), (1,)), ((), ())), preferred_element_type=jnp.float32,
            )
        g = g.astype(jnp.bfloat16).astype(jnp.float32).T
        grad[pl.ds(i * part, part)] = g.reshape(part, TILE, width)
        return carry

    lax.fori_loop(0, 3, multiply, 0)

    def pack(p):
        b = tile_ref[p]
        g = grad[b]
        first = 0.9 * one_ref[b] + 0.1 * g
        second = 0.999 * two_ref[b] + 0.001 * g * g
        step = first * (rate / bias_one) / (jnp.sqrt(second * (1.0 / bias_two)) + 1e-08)
        weight = (w_ref[b].astype(jnp.float32) - step).astype(jnp.bfloat16)
        qf, pf = fixed_point(first)
        qs, ps = fixed_point(second)
        cw = code_of(weight.astype(jnp.float32))
        outbox[p, :, 0:full] = qf[:, :full].astype(jnp.int16)
        outbox[p, :, full:2 * full] = qs[:, :full].astype(jnp.int16)
        outbox[p, :, 2 * full:3 * full] = cw[:, :full].astype(jnp.int16)
        lane = lax.broadcasted_iota(jnp.int32, (TILE, 128 - 3 * rest), 1)
        powers = jnp.where(lane == 0, pf, ps)
        end = jnp.concatenate([qf[:, full:], qs[:, full:], cw[:, full:], powers], axis=1)
        outbox[p, :, 3 * full:] = end.astype(jnp.int16)

    def copy_to(p, step):
        return pltpu.make_async_remote_copy(
            src_ref=outbox.at[p], dst_ref=inbox_ref.at[w],
            send_sem=send_sem.at[step], recv_sem=recv_sem.at[step],
            device_id=(n, p), device_id_type=MESH,
        )

    def send(i, carry):
        p, step = peer_of(i)
        pack(p)
        copy_to(p, step).start()
        return carry

    lax.fori_loop(1, AHEAD, send, 0)

    def partial(k, half):
        node = lax.rem(high + half, 2) * NX + lax.rem(x + k, NX)
        at = pl.ds(pl.multiple_of(node * tokens, tokens), tokens)
        share[k, half] = jnp.dot(wt_ref[...], f_ref[:, at], preferred_element_type=jnp.float32)

    x_copies = []
    for k in range(1, NX):
        for half in range(2):
            partial(k, half)
        copy = pltpu.make_async_remote_copy(
            src_ref=share.at[k], dst_ref=got.at[k - 1],
            send_sem=xs.at[k - 1], recv_sem=xr.at[k - 1],
            device_id=x_peers[k - 1], device_id_type=MESH,
        )
        copy.start()
        x_copies.append(copy)
    lax.fori_loop(AHEAD, many, send, 0)
    for half in range(2):
        partial(0, half)
    pack(w)
    mine = pltpu.make_async_copy(outbox.at[w], inbox_ref.at[w], loc)
    mine.start()

    blocks = grad.shape[0]
    lane = lax.broadcasted_iota(jnp.int32, (many, 128), 1)
    tables = t_ref[...].reshape((many,) + t_ref.shape[3:])
    ours = jnp.logical_and(tables[:, 0, :] == w, lane < blocks)
    slot = jnp.min(jnp.where(ours, tables[:, 1, :], 128), axis=1, keepdims=True)
    source = lax.broadcasted_iota(jnp.int32, (many, 128), 0)
    from_ref[...] = jnp.max(jnp.where(slot == lane, source, -1), axis=0, keepdims=True)

    for copy in x_copies:
        copy.wait_recv()
    total[...] = share[0, 1] + got[0, 1] + got[1, 1] + got[2, 1]
    across = pltpu.make_async_remote_copy(
        src_ref=total, dst_ref=across_got, send_sem=acs, recv_sem=acr,
        device_id=partner, device_id_type=MESH,
    )
    across.start()
    near = share[0, 0] + got[0, 0] + got[1, 0] + got[2, 0]
    across.wait_recv()
    out_ref[...] = (near + across_got[...]).astype(jnp.bfloat16)

    def finish(i, carry):
        p, step = peer_of(i)
        copy_to(p, step).wait()
        return carry

    lax.fori_loop(1, many, finish, 0)
    mine.wait()
    across.wait_send()
    for copy in x_copies:
        copy.wait_send()


def step_kernel(*refs):
    ins, outs, held, rest = refs[:8], refs[8:11], refs[11:25], refs[25:]
    (a_ref, b_ref, t_ref, tile_ref, call_ref, w_ref, one_ref, two_ref,
     owner_ref, slot_ref, x_ref, wt_ref, onet_ref, twot_ref) = held
    gather_part(*ins, *held, *rest[:23])
    exchange_part(
        tile_ref, a_ref, b_ref, t_ref, call_ref, wt_ref, w_ref, one_ref, two_ref,
        *outs, *rest[23:],
    )


def step(owners, slots, features, cotangent, wt, onet, twot):
    rows = features.shape[0]
    width, tokens = cotangent.shape
    depth = wt.shape[1]
    half = NY // 2
    pad = rows + rows // 3
    peers = NZ * NY * NC
    blocks = depth // TILE
    lanes = 3 * (width // 128 * 128) + 128
    i16, i32, f32, bf16 = jnp.int16, jnp.int32, jnp.float32, jnp.bfloat16
    return pl.pallas_call(
        step_kernel,
        out_shape=(
            jax.ShapeDtypeStruct((peers, TILE, lanes), i16),
            jax.ShapeDtypeStruct((width, tokens), bf16),
            jax.ShapeDtypeStruct((1, 128), i32),
        ),
        in_specs=[SMEM] + [HBM] * 7,
        out_specs=(VMEM,) * 3,
        scratch_shapes=[
            pltpu.VMEM((NZ, NY, NC, pad, HEAD), bf16),
            pltpu.VMEM((NZ, NY, NC, pad, KEEP - HEAD), bf16),
            pltpu.VMEM((NZ, NY, NC, 8, 128), i32),
            pltpu.SMEM((peers,), i32),
            pltpu.VMEM((NN, width, tokens), bf16),
            pltpu.VMEM((blocks, TILE, width), bf16),
            pltpu.VMEM((blocks, TILE, width), f32),
            pltpu.VMEM((blocks, TILE, width), f32),
            pltpu.VMEM(owners.shape, i32),
            pltpu.VMEM(slots.shape, i32),
            pltpu.VMEM(features.shape, bf16),
            pltpu.VMEM((width, depth), bf16),
            pltpu.VMEM((width, depth), f32),
            pltpu.VMEM((width, depth), f32),
            DMA((NZ - 1,)), DMA((NZ - 1,)),
            DMA((half, NZ)), DMA((half, NZ)),
            DMA((half, NZ)), DMA((half, NZ)),
            DMA((NY + 1,)), DMA((NY + 1,)),
            DMA((NY - 1,)), DMA((NY - 1,)),
            DMA((NZ - 1,)), DMA((NZ - 1,)),
            DMA((NZ,)), DMA((NZ,)),
            DMA((NY - 1,)), DMA((NY - 1,)),
            DMA((NZ - 1,)), DMA((NZ - 1,)),
            DMA((NZ,)), DMA((NZ,)),
            DMA((NN - 1,)), DMA((NN - 1,)),
            DMA((7,)),
            pltpu.VMEM((depth, tokens * NN), bf16),
            pltpu.VMEM((blocks, TILE, width), f32),
            pltpu.VMEM((peers, TILE, lanes), i16),
            pltpu.VMEM((NX, 2, width, tokens), f32),
            pltpu.VMEM((NX - 1, 2, width, tokens), f32),
            pltpu.VMEM((width, tokens), f32),
            pltpu.VMEM((width, tokens), f32),
            DMA((peers,)), DMA((peers,)),
            DMA((NX - 1,)), DMA((NX - 1,)),
            DMA, DMA, DMA,
        ],
        compiler_params=pltpu.CompilerParams(
            collective_id=0, has_side_effects=True, vmem_limit_bytes=48 * 1024 * 1024
        ),
        name="gather_update_exchange",
    )(owners, *(
        pltpu.with_memory_space_constraint(v, pltpu.HBM)
        for v in (owners, slots, features, cotangent, wt, onet, twot)
    ))


PER = 4


def place_kernel(
    from_ref, inbox_ref, total_ref, weight_out, first_out, second_out, out_ref,
    weight_ref, first_ref, second_ref, sems, last,
):
    capacity, _, width = weight_ref.shape
    full = width // 128 * 128
    rest = width - full
    whole = pltpu.make_async_copy(total_ref, out_ref, last)
    whole.start()

    def writes(i):
        at = pl.ds(i * PER, PER)
        return [
            pltpu.make_async_copy(ref.at[at], out.at[0, at], sems.at[k, i])
            for k, (ref, out) in enumerate((
                (first_ref, first_out), (second_ref, second_out), (weight_ref, weight_out),
            ))
        ]

    def some(i, carry):
        for j in range(PER):
            s = i * PER + j
            p = from_ref[0, s]
            q = jnp.where(p >= 0, inbox_ref[jnp.maximum(p, 0)].astype(jnp.int32), 0)
            end = q[:, 3 * full:]
            pf = jnp.exp2(end[:, 3 * rest:3 * rest + 1].astype(jnp.float32)) * (1.0 / TOP)
            ps = jnp.exp2(end[:, 3 * rest + 1:3 * rest + 2].astype(jnp.float32)) * (1.0 / TOP)
            first_ref[s, :, :full] = q[:, :full].astype(jnp.float32) * pf
            first_ref[s, :, full:] = end[:, :rest].astype(jnp.float32) * pf
            second_ref[s, :, :full] = q[:, full:2 * full].astype(jnp.float32) * ps
            second_ref[s, :, full:] = end[:, rest:2 * rest].astype(jnp.float32) * ps
            weight_ref[s, :, :full] = value_of(q[:, 2 * full:3 * full]).astype(jnp.bfloat16)
            weight_ref[s, :, full:] = value_of(end[:, 2 * rest:3 * rest]).astype(jnp.bfloat16)
        for copy in writes(i):
            copy.start()
        return carry

    lax.fori_loop(0, capacity // PER, some, 0)

    def finish(i, carry):
        for copy in writes(i):
            copy.wait()
        return carry

    lax.fori_loop(0, capacity // PER, finish, 0)
    whole.wait()


def place(source, inbox, total, capacity):
    shape = (1, capacity, TILE, total.shape[0])
    bf16, f32 = jnp.bfloat16, jnp.float32
    return pl.pallas_call(
        place_kernel,
        out_shape=(
            pltpu.HBM(shape, bf16),
            pltpu.HBM(shape, f32),
            pltpu.HBM(shape, f32),
            pltpu.HBM(total.shape, total.dtype),
        ),
        in_specs=[SMEM, VMEM, VMEM],
        out_specs=(HBM,) * 4,
        scratch_shapes=[
            pltpu.VMEM(shape[1:], bf16),
            pltpu.VMEM(shape[1:], f32),
            pltpu.VMEM(shape[1:], f32),
            DMA((3, capacity // PER)),
            DMA,
        ],
        compiler_params=pltpu.CompilerParams(vmem_limit_bytes=32 * 1024 * 1024),
        name="place_tiles",
    )(source, inbox, total)


def on_device(features, weight, moment_one, moment_two, cotangent, new_owner, new_slot):
    blocks = new_owner.shape[2]
    capacity = blocks + blocks // 6
    inbox, total, source = step(
        new_owner[0], new_slot[0], features, cotangent.T, weight.T, moment_one.T, moment_two.T
    )
    *moved, projected = place(source, inbox, total, capacity)
    return (projected.T,) + tuple(moved)


def solution(mesh):
    placed = (
        P(("node", "wide"), None),
        P("node", "wide"),
        P("node", "wide"),
        P("node", "wide"),
        P("node", "wide"),
        P("node", "wide", None),
        P("node", "wide", None),
    )
    return jax.shard_map(
        on_device,
        mesh=mesh,
        in_specs=placed,
        out_specs=(
            P("node", "wide"),
            P("node", "wide", None, None),
            P("node", "wide", None, None),
            P("node", "wide", None, None),
        ),
        check_vma=False,
    )
```

```python
import jax
import jax.numpy as jnp
from jax import lax
from jax.experimental import pallas as pl
from jax.experimental.pallas import tpu as pltpu
from jax.sharding import PartitionSpec as P

TILE = 32
NZ, NY, NC = 4, 8, 2
NX = 4
NN = 2 * NX
MESH = pl.DeviceIdType.MESH
ANY = pl.BlockSpec(memory_space=pl.ANY)
HBM = pl.BlockSpec(memory_space=pltpu.HBM)
VMEM = pl.BlockSpec(memory_space=pltpu.VMEM)
SMEM = pl.BlockSpec(memory_space=pltpu.SMEM)
DMA = pltpu.SemaphoreType.DMA

rate = 0.02
bias_one = 1.0 - 0.9**10
bias_two = 1.0 - 0.999**10

TOP = 32767.0
LEAST = 2.0**-100


def place_of(w):
    return w // (NY * NC), (w // NC) % NY, w % NC


def node_peers_of(n, w):
    x = lax.rem(n, NX)
    base = n - x
    return (lax.rem(n + NX, NN), w), [(base + lax.rem(x + k, NX), w) for k in range(1, NX)]


HEAD = 1280
AHEAD = 9
KEEP = 1536


def gather_part(
    owner_smem, owner_in, slot_in, x_in, c_in, wt_in, onet_in, twot_in,
    a_ref, b_ref, t_ref, tile_ref, call_ref, w_ref, one_ref, two_ref,
    owner_ref, slot_ref, x_ref, wt_ref, onet_ref, twot_ref,
    zs, zr, rs, rr, ls, lr, ss, sr, bs, br, bzs, bzr, bss, bsr,
    ts, tr, tzs, tzr, tss, tsr, ns, nr, loc,
):
    n = lax.axis_index("node")
    w = lax.axis_index("wide")
    z, y, c = place_of(w)

    def wide(zz, yy, cc):
        return (n, (lax.rem(zz + NZ, NZ) * NY + lax.rem(yy + NY, NY)) * NC + cc)

    sibling = wide(z, y, 1 - c)
    y_peers = [wide(z, y + k, c) for k in range(1, NY)]
    right, left = y_peers[0], y_peers[-1]
    z_peers = [wide(z + k, y, c) for k in range(1, NZ)]
    partner, x_peers = node_peers_of(n, w)

    barrier = pltpu.get_barrier_semaphore()
    for peer in [partner] + x_peers:
        pl.semaphore_signal(barrier, inc=1, device_id=peer, device_id_type=MESH)
    many = NZ * NY * NC

    def greet(i, carry):
        pl.semaphore_signal(
            barrier, inc=1, device_id=(n, lax.rem(w + i, many)), device_id_type=MESH
        )
        return carry

    lax.fori_loop(1, many, greet, 0)

    own = [
        pltpu.make_async_copy(src, dst, loc.at[i])
        for i, (src, dst) in enumerate((
            (x_in, x_ref), (c_in, call_ref.at[n]),
            (onet_in, onet_ref), (twot_in, twot_ref), (wt_in, wt_ref),
            (owner_in, owner_ref), (slot_in, slot_ref),
        ))
    ]
    for copy in own:
        copy.start()
    own[0].wait()

    rows = x_ref.shape[0]
    extra = x_ref.shape[1] - KEEP
    third = HEAD - 2 * extra
    a_ref[z, y, c, :rows, :] = x_ref[:, :HEAD]
    b_ref[z, y, c, :rows, :] = x_ref[:, HEAD:KEEP]
    for k in range(2):
        a_ref[z, y, c, rows:, k * extra:(k + 1) * extra] = x_ref[4 * k:4 * k + 4, KEEP:]
    a_ref[z, y, c, rows:, 2 * extra:] = x_ref[rows - 4:, KEEP:KEEP + third]
    b_ref[z, y, c, rows:, :] = x_ref[rows - 4:, KEEP + third:]
    own[5].wait()
    own[6].wait()
    t_ref[z, y, c, 0:1, :owner_ref.shape[1]] = owner_ref[...]
    t_ref[z, y, c, 1:2, :slot_ref.shape[1]] = slot_ref[...]
    own[1].wait()

    pl.semaphore_wait(barrier, many - 1 + NX)

    def send(ref, s, r, peer):
        copy = pltpu.make_async_remote_copy(
            src_ref=ref, dst_ref=ref, send_sem=s, recv_sem=r,
            device_id=peer, device_id_type=MESH,
        )
        copy.start()
        return copy

    b_copies = [
        send(b_ref.at[z, y, c], bs.at[k], br.at[k], y_peers[k]) for k in range(NY - 1)
    ]
    z_copies = [
        send(a_ref.at[z, y, c], zs.at[k], zr.at[k], z_peers[k]) for k in range(NZ - 1)
    ]
    across = send(call_ref.at[n], ns.at[0], nr.at[0], partner)
    x_copies = [
        send(call_ref.at[n], ns.at[k + 1], nr.at[k + 1], x_peers[k]) for k in range(NX - 1)
    ]
    t_copies = [
        send(t_ref.at[z, y, c], ts.at[k], tr.at[k], y_peers[k]) for k in range(NY - 1)
    ]

    def block(k, yy):
        return a_ref.at[lax.rem(z + k, NZ), lax.rem(yy + NY, NY), c]

    half = NY // 2
    order = (0, NZ - 1, 1, 2)
    from_left, from_right, to_sib = {}, {}, []
    for s in range(half + 1):
        for i, k in enumerate(order):
            if s == 0:
                if k > 0:
                    z_copies[NZ - k - 1].wait_recv()
            else:
                if (s - 1, k) in from_left:
                    from_left[s - 1, k].wait_recv()
                if (s - 1, k) in from_right:
                    from_right[s - 1, k].wait_recv()
            if s < half:
                last = s == half - 1
                if not last or i % 2 == 0:
                    from_left[s, k] = send(block(k, y - s), rs.at[s, k], rr.at[s, k], right)
                if not last or i % 2 == 1:
                    from_right[s, k] = send(block(k, y + s), ls.at[s, k], lr.at[s, k], left)
            if s == 0 and k == 0:
                for copy in b_copies:
                    copy.wait_recv()
                bz = [
                    send(b_ref.at[z, :, c], bzs.at[j], bzr.at[j], z_peers[j])
                    for j in range(NZ - 1)
                ]
        to_sib.append(send(a_ref.at[:, lax.rem(y - s + NY, NY), c], ss.at[2 * s], sr.at[2 * s], sibling))
        if 0 < s < half:
            to_sib.append(
                send(a_ref.at[:, lax.rem(y + s, NY), c], ss.at[2 * s - 1], sr.at[2 * s - 1], sibling)
            )
        if s == 0:
            sib_b = [send(b_ref.at[z, :, c], bss.at[0], bsr.at[0], sibling)]
            def tile_at(p, carry):
                tile = 0
                for t in range(owner_ref.shape[1]):
                    tile = jnp.where(owner_smem[0, t] == p, t, tile)
                tile_ref[p] = tile
                return carry

            lax.fori_loop(0, many, tile_at, 0)
            own[2].wait()
            one_ref[...] = onet_ref[...].T.reshape(one_ref.shape)
        if s == 1:
            across.wait_recv()
            other = call_ref.at[lax.rem(n + NX, NN)]
            x_copies += [
                send(other, ns.at[k + NX], nr.at[k + NX], x_peers[k]) for k in range(NX - 1)
            ]
            for copy in t_copies:
                copy.wait_recv()
            tz = [
                send(t_ref.at[z, :, c], tzs.at[k], tzr.at[k], z_peers[k]) for k in range(NZ - 1)
            ]
            sib_t = [send(t_ref.at[z, :, c], tss.at[0], tsr.at[0], sibling)]
            own[3].wait()
            two_ref[...] = twot_ref[...].T.reshape(two_ref.shape)
        if s == 2:
            own[4].wait()
            w_ref[...] = wt_ref[...].T.reshape(w_ref.shape)
    for k in (NZ - 1, 1, 2):
        at = lax.rem(z + k, NZ)
        bz[NZ - k - 1].wait_recv()
        sib_b.append(send(b_ref.at[at, :, c], bss.at[k], bsr.at[k], sibling))
        tz[NZ - k - 1].wait_recv()
        sib_t.append(send(t_ref.at[at, :, c], tss.at[k], tsr.at[k], sibling))

    for copy in z_copies + b_copies + t_copies + bz + tz + [across]:
        copy.wait_send()
    for copy in list(from_left.values()) + list(from_right.values()):
        copy.wait_send()
    for copy in to_sib + sib_b + sib_t + x_copies:
        copy.wait()


def arrange(a_ref, b_ref, f_ref):
    pad = a_ref.shape[3]
    rows = pad * 3 // 4
    extra = f_ref.shape[1] - KEEP

    def four(i, carry):
        at = pl.ds(pl.multiple_of(i * 4 * rows, 16), 4 * rows)
        ys = pl.ds(lax.rem(i, NY // 2) * 2, 2)
        a = a_ref[i // (NY // 2), ys]
        b = b_ref[i // (NY // 2), ys]
        a = a.reshape((4,) + a.shape[2:])
        b = b.reshape((4,) + b.shape[2:])
        f_ref[at, :HEAD] = jnp.concatenate([a[j, :rows] for j in range(4)], axis=0)
        f_ref[at, HEAD:KEEP] = jnp.concatenate([b[j, :rows] for j in range(4)], axis=0)
        ends = []
        for j in range(4):
            for k in range(2):
                ends.append(a[j, rows:, k * extra:(k + 1) * extra])
            ends.append(jnp.concatenate([a[j, rows:, 2 * extra:], b[j, rows:]], axis=1))
        f_ref[at, KEEP:] = jnp.concatenate(ends, axis=0)
        return carry

    lax.fori_loop(0, NZ * NY * NC // 4, four, 0, unroll=4)


def fixed_point(x):
    most = jnp.maximum(jnp.max(jnp.abs(x), axis=1, keepdims=True), LEAST)
    power = jnp.ceil(jnp.log2(most))
    q = jnp.round(x * (TOP * jnp.exp2(-power)))
    return jnp.clip(q, -TOP, TOP).astype(jnp.int32), power.astype(jnp.int32)


def code_of(x):
    a = jnp.abs(x)
    some = a >= 2.0**-126
    safe = jnp.where(some, a, 1.0)
    e = jnp.floor(jnp.log2(safe))
    code = jnp.round((e + 127.0) * 128.0 + (safe * jnp.exp2(-e) - 1.0) * 128.0)
    code = jnp.where(some, code, 0.0)
    return jnp.where(x < 0.0, -code, code).astype(jnp.int32)


def value_of(code):
    a = jnp.abs(code)
    e = lax.shift_right_logical(a, 7)
    m = lax.bitwise_and(a, 127)
    v = (1.0 + m.astype(jnp.float32) * (1.0 / 128.0)) * jnp.exp2(e.astype(jnp.float32) - 127.0)
    v = jnp.where(a == 0, 0.0, v)
    return jnp.where(code < 0, -v, v)


def exchange_part(
    tile_ref, a_ref, b_ref, t_ref, c_ref, wt_ref, w_ref, one_ref, two_ref,
    inbox_ref, out_ref, from_ref, f_ref, grad, outbox, share, got, total, across_got,
    send_sem, recv_sem, xs, xr, acs, acr, loc,
):
    n = lax.axis_index("node")
    w = lax.axis_index("wide")
    many = outbox.shape[0]
    partner, x_peers = node_peers_of(n, w)
    width = w_ref.shape[2]
    full = width // 128 * 128
    rest = width - full

    z, y, c = place_of(w)
    x, high = lax.rem(n, NX), n // NX

    def peer_of(i):
        step = lax.rem(i * 45, many)
        sign = 1 - 2 * c
        dz, dy, dc = place_of(step)
        to_z = lax.rem(z + NZ + sign * dz, NZ)
        to_y = lax.rem(y + NY + sign * dy, NY)
        return (to_z * NY + to_y) * NC + lax.rem(c + dc, NC), step

    arrange(a_ref, b_ref, f_ref)
    part = grad.shape[0] // 3
    tokens = c_ref.shape[2]

    def multiply(i, carry):
        at = pl.ds(pl.multiple_of(i * part * TILE, 256), part * TILE)
        g = jnp.zeros((width, part * TILE), jnp.float32)
        for k in range(c_ref.shape[0]):
            g += lax.dot_general(
                c_ref[k], f_ref[at, k * tokens:(k + 1) * tokens],
                (((1,), (1,)), ((), ())), preferred_element_type=jnp.float32,
            )
        g = g.astype(jnp.bfloat16).astype(jnp.float32).T
        grad[pl.ds(i * part, part)] = g.reshape(part, TILE, width)
        return carry

    lax.fori_loop(0, 3, multiply, 0, unroll=True)

    def pack(p):
        b = tile_ref[p]
        g = grad[b]
        first = 0.9 * one_ref[b] + 0.1 * g
        second = 0.999 * two_ref[b] + 0.001 * g * g
        step = first * (rate / bias_one) / (jnp.sqrt(second * (1.0 / bias_two)) + 1e-08)
        weight = (w_ref[b].astype(jnp.float32) - step).astype(jnp.bfloat16)
        qf, pf = fixed_point(first)
        qs, ps = fixed_point(second)
        cw = code_of(weight.astype(jnp.float32))
        outbox[p, :, 0:full] = qf[:, :full].astype(jnp.int16)
        outbox[p, :, full:2 * full] = qs[:, :full].astype(jnp.int16)
        outbox[p, :, 2 * full:3 * full] = cw[:, :full].astype(jnp.int16)
        lane = lax.broadcasted_iota(jnp.int32, (TILE, 128 - 3 * rest), 1)
        powers = jnp.where(lane == 0, pf, ps)
        end = jnp.concatenate([qf[:, full:], qs[:, full:], cw[:, full:], powers], axis=1)
        outbox[p, :, 3 * full:] = end.astype(jnp.int16)

    def copy_to(p, step):
        return pltpu.make_async_remote_copy(
            src_ref=outbox.at[p], dst_ref=inbox_ref.at[w],
            send_sem=send_sem.at[step], recv_sem=recv_sem.at[step],
            device_id=(n, p), device_id_type=MESH,
        )

    def send(i, carry):
        p, step = peer_of(i)
        pack(p)
        copy_to(p, step).start()
        return carry

    lax.fori_loop(1, AHEAD, send, 0)

    def partial(k, half):
        node = lax.rem(high + half, 2) * NX + lax.rem(x + k, NX)
        at = pl.ds(pl.multiple_of(node * tokens, tokens), tokens)
        share[k, half] = jnp.dot(wt_ref[...], f_ref[:, at], preferred_element_type=jnp.float32)

    x_copies = []
    for k in range(1, NX):
        for half in range(2):
            partial(k, half)
        copy = pltpu.make_async_remote_copy(
            src_ref=share.at[k], dst_ref=got.at[k - 1],
            send_sem=xs.at[k - 1], recv_sem=xr.at[k - 1],
            device_id=x_peers[k - 1], device_id_type=MESH,
        )
        copy.start()
        x_copies.append(copy)
    lax.fori_loop(AHEAD, many, send, 0)
    for half in range(2):
        partial(0, half)
    pack(w)
    mine = pltpu.make_async_copy(outbox.at[w], inbox_ref.at[w], loc)
    mine.start()

    blocks = grad.shape[0]
    lane = lax.broadcasted_iota(jnp.int32, (many, 128), 1)
    tables = t_ref[...].reshape((many,) + t_ref.shape[3:])
    ours = jnp.logical_and(tables[:, 0, :] == w, lane < blocks)
    slot = jnp.min(jnp.where(ours, tables[:, 1, :], 128), axis=1, keepdims=True)
    source = lax.broadcasted_iota(jnp.int32, (many, 128), 0)
    from_ref[...] = jnp.max(jnp.where(slot == lane, source, -1), axis=0, keepdims=True)

    for copy in x_copies:
        copy.wait_recv()
    total[...] = share[0, 1] + got[0, 1] + got[1, 1] + got[2, 1]
    across = pltpu.make_async_remote_copy(
        src_ref=total, dst_ref=across_got, send_sem=acs, recv_sem=acr,
        device_id=partner, device_id_type=MESH,
    )
    across.start()
    near = share[0, 0] + got[0, 0] + got[1, 0] + got[2, 0]
    across.wait_recv()
    out_ref[...] = (near + across_got[...]).astype(jnp.bfloat16)

    def finish(i, carry):
        p, step = peer_of(i)
        copy_to(p, step).wait()
        return carry

    lax.fori_loop(1, many, finish, 0)
    mine.wait()
    across.wait_send()
    for copy in x_copies:
        copy.wait_send()


def step_kernel(*refs):
    ins, outs, held, rest = refs[:8], refs[8:11], refs[11:25], refs[25:]
    (a_ref, b_ref, t_ref, tile_ref, call_ref, w_ref, one_ref, two_ref,
     owner_ref, slot_ref, x_ref, wt_ref, onet_ref, twot_ref) = held
    gather_part(*ins, *held, *rest[:23])
    exchange_part(
        tile_ref, a_ref, b_ref, t_ref, call_ref, wt_ref, w_ref, one_ref, two_ref,
        *outs, *rest[23:],
    )


def step(owners, slots, features, cotangent, wt, onet, twot):
    rows = features.shape[0]
    width, tokens = cotangent.shape
    depth = wt.shape[1]
    half = NY // 2
    pad = rows + rows // 3
    peers = NZ * NY * NC
    blocks = depth // TILE
    lanes = 3 * (width // 128 * 128) + 128
    i16, i32, f32, bf16 = jnp.int16, jnp.int32, jnp.float32, jnp.bfloat16
    return pl.pallas_call(
        step_kernel,
        out_shape=(
            jax.ShapeDtypeStruct((peers, TILE, lanes), i16),
            jax.ShapeDtypeStruct((width, tokens), bf16),
            jax.ShapeDtypeStruct((1, 128), i32),
        ),
        in_specs=[SMEM] + [HBM] * 7,
        out_specs=(VMEM,) * 3,
        scratch_shapes=[
            pltpu.VMEM((NZ, NY, NC, pad, HEAD), bf16),
            pltpu.VMEM((NZ, NY, NC, pad, KEEP - HEAD), bf16),
            pltpu.VMEM((NZ, NY, NC, 8, 128), i32),
            pltpu.SMEM((peers,), i32),
            pltpu.VMEM((NN, width, tokens), bf16),
            pltpu.VMEM((blocks, TILE, width), bf16),
            pltpu.VMEM((blocks, TILE, width), f32),
            pltpu.VMEM((blocks, TILE, width), f32),
            pltpu.VMEM(owners.shape, i32),
            pltpu.VMEM(slots.shape, i32),
            pltpu.VMEM(features.shape, bf16),
            pltpu.VMEM((width, depth), bf16),
            pltpu.VMEM((width, depth), f32),
            pltpu.VMEM((width, depth), f32),
            DMA((NZ - 1,)), DMA((NZ - 1,)),
            DMA((half, NZ)), DMA((half, NZ)),
            DMA((half, NZ)), DMA((half, NZ)),
            DMA((NY + 1,)), DMA((NY + 1,)),
            DMA((NY - 1,)), DMA((NY - 1,)),
            DMA((NZ - 1,)), DMA((NZ - 1,)),
            DMA((NZ,)), DMA((NZ,)),
            DMA((NY - 1,)), DMA((NY - 1,)),
            DMA((NZ - 1,)), DMA((NZ - 1,)),
            DMA((NZ,)), DMA((NZ,)),
            DMA((NN - 1,)), DMA((NN - 1,)),
            DMA((7,)),
            pltpu.VMEM((depth, tokens * NN), bf16),
            pltpu.VMEM((blocks, TILE, width), f32),
            pltpu.VMEM((peers, TILE, lanes), i16),
            pltpu.VMEM((NX, 2, width, tokens), f32),
            pltpu.VMEM((NX - 1, 2, width, tokens), f32),
            pltpu.VMEM((width, tokens), f32),
            pltpu.VMEM((width, tokens), f32),
            DMA((peers,)), DMA((peers,)),
            DMA((NX - 1,)), DMA((NX - 1,)),
            DMA, DMA, DMA,
        ],
        compiler_params=pltpu.CompilerParams(
            collective_id=0, has_side_effects=True, vmem_limit_bytes=48 * 1024 * 1024
        ),
        name="gather_update_exchange",
    )(owners, *(
        pltpu.with_memory_space_constraint(v, pltpu.HBM)
        for v in (owners, slots, features, cotangent, wt, onet, twot)
    ))


PER = 4


def place_kernel(
    from_ref, inbox_ref, total_ref, weight_out, first_out, second_out, out_ref,
    weight_ref, first_ref, second_ref, sems, last,
):
    capacity, _, width = weight_ref.shape
    full = width // 128 * 128
    rest = width - full
    whole = pltpu.make_async_copy(total_ref, out_ref, last)
    whole.start()

    def writes(i):
        at = pl.ds(i * PER, PER)
        return [
            pltpu.make_async_copy(ref.at[at], out.at[0, at], sems.at[k, i])
            for k, (ref, out) in enumerate((
                (first_ref, first_out), (second_ref, second_out), (weight_ref, weight_out),
            ))
        ]

    def some(i, carry):
        for j in range(PER):
            s = i * PER + j
            p = from_ref[0, s]
            q = jnp.where(p >= 0, inbox_ref[jnp.maximum(p, 0)].astype(jnp.int32), 0)
            end = q[:, 3 * full:]
            pf = jnp.exp2(end[:, 3 * rest:3 * rest + 1].astype(jnp.float32)) * (1.0 / TOP)
            ps = jnp.exp2(end[:, 3 * rest + 1:3 * rest + 2].astype(jnp.float32)) * (1.0 / TOP)
            first_ref[s, :, :full] = q[:, :full].astype(jnp.float32) * pf
            first_ref[s, :, full:] = end[:, :rest].astype(jnp.float32) * pf
            second_ref[s, :, :full] = q[:, full:2 * full].astype(jnp.float32) * ps
            second_ref[s, :, full:] = end[:, rest:2 * rest].astype(jnp.float32) * ps
            weight_ref[s, :, :full] = value_of(q[:, 2 * full:3 * full]).astype(jnp.bfloat16)
            weight_ref[s, :, full:] = value_of(end[:, 2 * rest:3 * rest]).astype(jnp.bfloat16)
        for copy in writes(i):
            copy.start()
        return carry

    lax.fori_loop(0, capacity // PER, some, 0)

    def finish(i, carry):
        for copy in writes(i):
            copy.wait()
        return carry

    lax.fori_loop(0, capacity // PER, finish, 0)
    whole.wait()


def place(source, inbox, total, capacity):
    shape = (1, capacity, TILE, total.shape[0])
    bf16, f32 = jnp.bfloat16, jnp.float32
    return pl.pallas_call(
        place_kernel,
        out_shape=(
            pltpu.HBM(shape, bf16),
            pltpu.HBM(shape, f32),
            pltpu.HBM(shape, f32),
            pltpu.HBM(total.shape, total.dtype),
        ),
        in_specs=[SMEM, VMEM, VMEM],
        out_specs=(HBM,) * 4,
        scratch_shapes=[
            pltpu.VMEM(shape[1:], bf16),
            pltpu.VMEM(shape[1:], f32),
            pltpu.VMEM(shape[1:], f32),
            DMA((3, capacity // PER)),
            DMA,
        ],
        compiler_params=pltpu.CompilerParams(vmem_limit_bytes=32 * 1024 * 1024),
        name="place_tiles",
    )(source, inbox, total)


def on_device(features, weight, moment_one, moment_two, cotangent, new_owner, new_slot):
    blocks = new_owner.shape[2]
    capacity = blocks + blocks // 6
    inbox, total, source = step(
        new_owner[0], new_slot[0], features, cotangent.T, weight.T, moment_one.T, moment_two.T
    )
    *moved, projected = place(source, inbox, total, capacity)
    return (projected.T,) + tuple(moved)


def solution(mesh):
    placed = (
        P(("node", "wide"), None),
        P("node", "wide"),
        P("node", "wide"),
        P("node", "wide"),
        P("node", "wide"),
        P("node", "wide", None),
        P("node", "wide", None),
    )
    return jax.shard_map(
        on_device,
        mesh=mesh,
        in_specs=placed,
        out_specs=(
            P("node", "wide"),
            P("node", "wide", None, None),
            P("node", "wide", None, None),
            P("node", "wide", None, None),
        ),
        check_vma=False,
    )
```
